32 devices in a mesh: req: 8 (over y, x, core), mesh: 4 (over z).
Axes of the slice: x: 2, y: 2, z: 4, core: 2. Of those that a mesh axis runs over, the one named last changes fastest.
Arguments:
- tokens: bfloat16 [128, 64, 1024], P(('req', 'mesh')), may hold values from -6 to 6
- lengths: int32 [128], P(('req', 'mesh')), may hold values from 1 to 64, 6144 in all
- ridge_keys: float32 [128, 8, 128, 128], P(('req', 'mesh')), as said below
- ridge_values: float32 [128, 8, 128, 128], P(('req', 'mesh')), may hold values from -0.5 to 0.5
- conv_tail: bfloat16 [128, 3, 3072], P(('req', 'mesh')), may hold values from -6 to 6
- page_table: int32 [128], P(('req', 'mesh')), may hold values from 0 to 15, as said below
- w_qkv: bfloat16 [1024, 3072], P(('req', 'mesh')), may hold values from -0.1875 to 0.1875
- conv_weight: float32 [4, 3072], replicated, may hold values from -3 to 3
- w_gates: bfloat16 [1024, 16], replicated, may hold values from -0.1875 to 0.1875
- decay_rate: float32 [8], replicated, may hold values from 0.001 to 0.03
- ridge: float32 [8], replicated, may hold values from 0.01 to 0.1
- w_out: bfloat16 [1024, 1024], P(('req', 'mesh')), may hold values from -0.1875 to 0.1875
- attn_gain: float32 [1024], replicated, may hold values from 0.5 to 1.5
- ffn_gain: float32 [1024], replicated, may hold values from 0.5 to 1.5
- w_gate: bfloat16 [1024, 2816], P('req', 'mesh'), may hold values from -0.1875 to 0.1875
- w_up: bfloat16 [1024, 2816], P('req', 'mesh'), may hold values from -0.1875 to 0.1875
- w_down: bfloat16 [2816, 1024], P('mesh', 'req'), may hold values from -0.109375 to 0.109375
Outputs:
- mixed: bfloat16 [128, 64, 1024], P(('req', 'mesh'))
- keys_decode: float32 [128, 8, 128, 128], P(('req', 'mesh'))
- values_decode: float32 [128, 8, 128, 128], P(('req', 'mesh'))
- tail_decode: bfloat16 [128, 3, 3072], P(('req', 'mesh'))
- readout: bfloat16 [128, 64, 1024], P(('req', 'mesh'))
The draws below stay inside these ranges and needn't reach their ends.
Inputs may be any that keep to these rules, and one draw needn't show every extreme that they name: `page_table`: within each group of 16 consecutive requests the values are a permutation; value // 4 is a decode device of the group and value % 4 a slot on it, and the 4 requests of one device go to 4 different decode devices. `ridge_keys`: each matrix is symmetric with a positive diagonal that exceeds the sum of the magnitudes of its row's other entries.
All inputs are finite; a program needn't handle non-finite values. No bound on the sum of `lengths` on one device may be relied on, other than what follows from the above.
Results may differ from the reference program's by a relative error of at most 0.0095.
Values may be sent and summed in bfloat16 or wider, within the bound.
No kernel may reach another device: no remote copies, remote signals or barrier semaphores. Data moves between devices by JAX's collectives and lax.ppermute only.
A program may use at most 128 MiB of HBM per device.

```python
import math
import jax
import jax.numpy as jnp
import numpy as np
from jax import lax

D = 1024
HEADS = 8
HEAD_DIM = 128
FF = 2816
CONV = 4
ITERS = 5
SPAN = 64
R_DEV = 4
REQS = 128


def draw_ridge_keys(key, part):
    first_key, second_key = jax.random.split(jax.random.fold_in(key, 11))
    unit_off = jax.random.uniform(first_key, (REQS, HEADS, HEAD_DIM, HEAD_DIM), jnp.float32, -1.0, 1.0)
    unit_off = 0.5 * (unit_off + jnp.swapaxes(unit_off, 2, 3))
    fraction = jax.random.uniform(second_key, (REQS, HEADS, HEAD_DIM), jnp.float32)
    diagonal = 0.05 * jnp.exp(jnp.log(100.0) * fraction)
    smaller = jnp.minimum(diagonal[..., :, None], diagonal[..., None, :])
    symmetric = unit_off * smaller / HEAD_DIM
    position = jnp.arange(HEAD_DIM, dtype=jnp.int32)
    identity = position[:, None] == position[None, :]
    return jnp.where(identity, diagonal[..., :, None], symmetric)


def draw_page_table(key, part):
    group_count = REQS // (R_DEV * R_DEV)
    first_key, second_key = jax.random.split(jax.random.fold_in(key, 23))
    dest_keys = jax.random.split(first_key, group_count * R_DEV)
    slot_keys = jax.random.split(second_key, group_count * R_DEV)
    destination = jax.vmap(lambda one_key: jax.random.permutation(one_key, R_DEV))(dest_keys).reshape(group_count, R_DEV, R_DEV)
    slot_order = jax.vmap(lambda one_key: jax.random.permutation(one_key, R_DEV))(slot_keys).reshape(group_count, R_DEV, R_DEV)
    by_source = jnp.swapaxes(slot_order, 1, 2)
    slot_index = jnp.take_along_axis(by_source, destination, axis=2)
    return (destination * R_DEV + slot_index).reshape(REQS).astype(jnp.int32)


def steps_of(own_key, dims, shards, least, top_value):
    level, own = 1.0, jax.random.fold_in(own_key, 6)
    for axis_at, shards_of in shards:
        draws = jnp.exp(jax.random.uniform(jax.random.fold_in(own, axis_at), (shards_of,), jnp.float32, least / len(shards), top_value / len(shards)))
        level = level * jnp.repeat(draws, dims[axis_at] // shards_of).reshape([-1 if axis == axis_at else 1 for axis in range(len(dims))])
    return level


def split_up(number_of, total, most, lean):
    portions = [(1 << 20) // math.isqrt(grade ** lean) + 1 for grade in range(2, number_of + 1)]
    surplus, given = total - most - (number_of - 1), [1] * (number_of - 1)
    while surplus > 0:
        movable = [i for i in range(number_of - 1) if given[i] < most]
        whole, left = sum([portions[i] for i in movable]), surplus
        for i in movable:
            addition = min(most - given[i], max(1, left * portions[i] // whole), surplus)
            given[i] = given[i] + addition
            surplus = surplus - addition
    return np.array([most] + given)


def ragged_sizes(rng, number_of, total, reach, skew):
    if number_of == 2:
        one = jax.random.randint(rng, (), max(1, total - reach), min(reach, total - 1) + 1)
        return jnp.stack([one, total - one])
    sizes = jnp.asarray(split_up(number_of, total, reach, skew), jnp.int32)
    pairs = (number_of - 1) // 2
    source_of, taker = sizes[1:1 + 2 * pairs:2], sizes[2:2 + 2 * pairs:2]
    margin = jnp.minimum(source_of - 1, reach - taker)
    shifted = jax.random.randint(jax.random.fold_in(rng, 1), (pairs,), 0, 1 << 20) % (margin + 1)
    sizes = sizes.at[1:1 + 2 * pairs:2].set(source_of - shifted).at[2:2 + 2 * pairs:2].set(taker + shifted)
    return sizes[jax.random.permutation(jax.random.fold_in(rng, 2), number_of)]


def scatter_about(stream_key, extent, scale, most, pieces=(), held_as=jnp.bfloat16):
    array = scale * jax.random.normal(stream_key, extent, jnp.float32)
    if pieces:
        array = array * steps_of(stream_key, extent, pieces, -0.22, 0.18)
    return jnp.clip(array, -most, most).astype(held_as)


def setup_inputs(seed: int = 0) -> dict:
    streams_of = jax.random.split(jax.random.key(seed), 18)
    return {
        "tokens": scatter_about(streams_of[0], (REQS, SPAN, D), 1.0, 6.0, ((0, 32),)),
        "lengths": ragged_sizes(streams_of[1], REQS, REQS * SPAN * 3 // 4, SPAN, 2).astype(jnp.int32),
        "ridge_keys": draw_ridge_keys(jax.random.fold_in(streams_of[17], 71), 0),
        "ridge_values": scatter_about(streams_of[3], (REQS, HEADS, HEAD_DIM, HEAD_DIM), HEAD_DIM ** -0.5, 0.5, ((0, 32),), jnp.float32),
        "conv_tail": scatter_about(streams_of[4], (REQS, CONV - 1, 3 * HEADS * HEAD_DIM), 1.0, 6.0, ((0, 32),)),
        "page_table": draw_page_table(jax.random.fold_in(streams_of[17], 71), 0),
        "w_qkv": scatter_about(streams_of[6], (D, 3 * HEADS * HEAD_DIM), D ** -0.5, 0.1875, ((0, 32),)),
        "conv_weight": scatter_about(streams_of[7], (CONV, 3 * HEADS * HEAD_DIM), CONV ** -0.5, 3.0, (), jnp.float32),
        "w_gates": scatter_about(streams_of[8], (D, 2 * HEADS), D ** -0.5, 0.1875),
        "decay_rate": jnp.clip(jnp.exp(jax.random.uniform(streams_of[9], (HEADS,), jnp.float32, math.log(0.001), math.log(0.03))), 0.001, 0.03),
        "ridge": jnp.clip(jnp.exp(jax.random.uniform(streams_of[10], (HEADS,), jnp.float32, math.log(0.01), math.log(0.1))), 0.01, 0.1),
        "w_out": scatter_about(streams_of[11], (HEADS * HEAD_DIM, D), (HEADS * HEAD_DIM) ** -0.5, 0.1875, ((0, 32),)),
        "attn_gain": jnp.clip(1.0 + 0.1 * jax.random.normal(streams_of[12], (D,), jnp.float32), 0.5, 1.5),
        "ffn_gain": jnp.clip(1.0 + 0.1 * jax.random.normal(streams_of[13], (D,), jnp.float32), 0.5, 1.5),
        "w_gate": scatter_about(streams_of[14], (D, FF), D ** -0.5, 0.1875, ((0, 8), (1, 4))),
        "w_up": scatter_about(streams_of[15], (D, FF), D ** -0.5, 0.1875, ((0, 8), (1, 4))),
        "w_down": scatter_about(streams_of[16], (FF, D), FF ** -0.5, 0.109375, ((0, 4), (1, 8))),
    }


def rms_norm(values, gain):
    return values * lax.rsqrt(lax.optimization_barrier(jnp.mean(values * values, axis=-1, keepdims=True)) + 1e-05) * gain

def unit_rows(values):
    return values * lax.rsqrt(lax.optimization_barrier(jnp.sum(values * values, axis=-1, keepdims=True)) + 1e-06)

def prepare_heads(projected, gate_logits, conv_tail, lengths, conv_weight, decay_rate):
    requests, length, columns = projected.shape
    heads = decay_rate.shape[0]
    window = conv_tail.shape[1]
    extended = jnp.concatenate([conv_tail, projected], axis=1)
    conv_sum = jnp.zeros((requests, length, columns), jnp.float32)
    for tap_index in range(window + 1):
        conv_sum = conv_sum + conv_weight[tap_index] * extended[:, tap_index:tap_index + length].astype(jnp.float32)
    activated = jax.nn.silu(conv_sum).reshape(requests, length, 3, heads, columns // (3 * heads))
    queries = unit_rows(activated[:, :, 0])
    keys_now = unit_rows(activated[:, :, 1])
    values_now = activated[:, :, 2]
    position = jnp.arange(length, dtype=jnp.int32)
    live = (position[None, :] < lengths[:, None]).astype(jnp.float32)[:, :, None]
    beta = jax.nn.sigmoid(gate_logits[..., 0]) * live
    log_decay = -decay_rate * jax.nn.softplus(gate_logits[..., 1]) * live
    new_tail = jax.vmap(lambda rows_all, first_row: lax.dynamic_slice_in_dim(rows_all, first_row, window, 0))(extended, lengths.astype(jnp.int32))
    return (queries, keys_now, values_now, beta, log_decay, new_tail)

def mesa_core(queries, keys_now, values_now, beta, log_decay, keys_start, values_start, ridge, iterations):
    highest = lax.Precision.HIGHEST
    cumulative = jnp.cumsum(jnp.swapaxes(log_decay, 1, 2), axis=-1)
    beta_heads = jnp.swapaxes(beta, 1, 2)
    length = cumulative.shape[-1]
    position = jnp.arange(length, dtype=jnp.int32)
    causal = position[:, None] >= position[None, :]
    spread = cumulative[..., :, None] - cumulative[..., None, :]
    weight = jnp.where(causal, jnp.exp(jnp.minimum(spread, 0.0)), 0.0) * beta_heads[..., None, :]
    carried = jnp.swapaxes(jnp.exp(cumulative), 1, 2)[..., None]
    ridge_term = ridge[None, None, :, None]

    def apply_system(field):
        start_part = carried * jnp.einsum('bthj,bhij->bthi', field, keys_start, precision=highest)
        scores = jnp.einsum('bthj,bshj->bhts', field, keys_now, precision=highest) * weight
        return start_part + jnp.einsum('bhts,bshj->bthj', scores, keys_now, precision=highest) + ridge_term * field
    solution = jnp.zeros_like(queries)
    residual = queries
    direction = queries
    res_norm = lax.optimization_barrier(jnp.sum(residual * residual, axis=-1, keepdims=True))
    for step_index in range(iterations):
        applied = apply_system(direction)
        step_size = res_norm / (lax.optimization_barrier(jnp.sum(direction * applied, axis=-1, keepdims=True)) + 1e-20)
        solution = solution + step_size * direction
        residual = residual - step_size * applied
        next_norm = lax.optimization_barrier(jnp.sum(residual * residual, axis=-1, keepdims=True))
        direction = residual + next_norm / (res_norm + 1e-20) * direction
        res_norm = next_norm
    read_start = carried * jnp.einsum('bthj,bhij->bthi', solution, values_start, precision=highest)
    scores = jnp.einsum('bthj,bshj->bhts', solution, keys_now, precision=highest) * weight
    readout = read_start + jnp.einsum('bhts,bshj->bthj', scores, values_now, precision=highest)
    tail_weight = jnp.swapaxes(jnp.exp(cumulative[..., -1:] - cumulative) * beta_heads, 1, 2)[..., None]
    final_decay = jnp.exp(cumulative[..., -1])[..., None, None]
    keys_end = final_decay * keys_start + jnp.einsum('bshi,bshj->bhij', keys_now * tail_weight, keys_now, precision=highest)
    values_end = final_decay * values_start + jnp.einsum('bshi,bshj->bhij', values_now * tail_weight, keys_now, precision=highest)
    return (readout, keys_end, values_end)

def layer_forward(tokens, lengths, keys_start, values_start, conv_tail, w_qkv, conv_weight, w_gates, decay_rate, ridge, w_out, attn_gain, ffn_gain, w_gate, w_up, w_down):
    requests, length, width = tokens.shape
    heads = decay_rate.shape[0]
    resident = tokens.astype(jnp.float32).reshape(requests * length, width)
    normed = rms_norm(resident, attn_gain).astype(jnp.bfloat16)
    projected = jnp.dot(normed, w_qkv, preferred_element_type=jnp.float32).astype(jnp.bfloat16).reshape(requests, length, -1)
    gate_logits = jnp.dot(normed, w_gates, preferred_element_type=jnp.float32).reshape(requests, length, heads, 2)
    queries, keys_now, values_now, beta, log_decay, new_tail = prepare_heads(projected, gate_logits, conv_tail, lengths, conv_weight, decay_rate)
    readout, keys_end, values_end = mesa_core(queries, keys_now, values_now, beta, log_decay, keys_start, values_start, ridge, ITERS)
    head_rows = readout.reshape(requests * length, -1).astype(jnp.bfloat16)
    attended = jnp.dot(head_rows, w_out, preferred_element_type=jnp.float32)
    after_attn = (resident + attended).astype(jnp.bfloat16)
    ffn_in = rms_norm(after_attn.astype(jnp.float32), ffn_gain).astype(jnp.bfloat16)
    gate_proj = jnp.dot(ffn_in, w_gate, preferred_element_type=jnp.float32)
    upward = jnp.dot(ffn_in, w_up, preferred_element_type=jnp.float32)
    hidden = (jax.nn.silu(gate_proj) * upward).astype(jnp.bfloat16)
    ffn_out = jnp.dot(hidden, w_down, preferred_element_type=jnp.float32)
    mixed = (after_attn.astype(jnp.float32) + ffn_out).astype(jnp.bfloat16).reshape(requests, length, width)
    return (mixed, keys_end, values_end, new_tail, head_rows.reshape(requests, length, -1))

def reference(tokens, lengths, ridge_keys, ridge_values, conv_tail, page_table, w_qkv, conv_weight, w_gates, decay_rate, ridge, w_out, attn_gain, ffn_gain, w_gate, w_up, w_down):
    block_size = 8
    block_count = REQS // block_size

    def split_blocks(values):
        return values.reshape((block_count, block_size) + values.shape[1:])

    def merge_blocks(values):
        return values.reshape((REQS,) + values.shape[2:])

    def one_block(block_items):
        tok_block, len_block, keys_block, vals_block, tail_block = block_items
        return layer_forward(tok_block, len_block, keys_block, vals_block, tail_block, w_qkv, conv_weight, w_gates, decay_rate, ridge, w_out, attn_gain, ffn_gain, w_gate, w_up, w_down)
    mixed, keys_end, values_end, new_tail, readout = lax.map(one_block, (split_blocks(tokens), split_blocks(lengths), split_blocks(ridge_keys), split_blocks(ridge_values), split_blocks(conv_tail)))
    mixed = merge_blocks(mixed)
    keys_end = merge_blocks(keys_end)
    values_end = merge_blocks(values_end)
    new_tail = merge_blocks(new_tail)
    readout = merge_blocks(readout)
    group_size = R_DEV * R_DEV
    target = jnp.arange(REQS, dtype=jnp.int32) // group_size * group_size + page_table.astype(jnp.int32)
    keys_decode = jnp.zeros_like(keys_end).at[target].set(keys_end)
    values_decode = jnp.zeros_like(values_end).at[target].set(values_end)
    tail_decode = jnp.zeros_like(new_tail).at[target].set(new_tail)
    return (mixed, keys_decode, values_decode, tail_decode, readout)
```

```python
import functools

import jax
import jax.numpy as jnp
import numpy as np
from jax import lax
from jax.experimental import pallas as pl
from jax.experimental.pallas import tpu as pltpu
from jax.sharding import PartitionSpec as P

ITERS = 5
AXES = ("req", "mesh")
F32 = jnp.float32
BF16 = jnp.bfloat16
TAIL_ROW = 5


def rms_norm(values, gain):
    return values * lax.rsqrt(jnp.mean(values * values, axis=-1, keepdims=True) + 1e-05) * gain


def cost(flops, bytes_accessed):
    return pl.CostEstimate(flops=flops, bytes_accessed=bytes_accessed, transcendentals=0)


def in_hbm(values):
    return [pltpu.with_memory_space_constraint(value, pltpu.HBM) for value in values]


def flip_req(bit, reqs, peers):
    return [(r * peers + z, (r ^ bit) * peers + z) for r in range(reqs) for z in range(peers)]


def shift_mesh(step, reqs, peers):
    return [(r * peers + z, r * peers + (z + step) % peers) for r in range(reqs) for z in range(peers)]


def flip_mesh(bit, reqs, peers):
    return [(r * peers + z, r * peers + (z ^ bit)) for r in range(reqs) for z in range(peers)]


def gather_rows(own, move, shifts, flips):
    flip_core, flip_x, flip_y = flips
    rows = own.shape[0]
    one = move(own, shifts[1])
    x_own, y_own = move(own, flip_x), move(own, flip_y)
    three = move(own, shifts[3])
    two = move(one, shifts[1])
    x_one, y_one = move(one, flip_x), move(one, flip_y)
    rest = jnp.concatenate([three, two], axis=0)
    x_rest, y_rest = move(rest, flip_x), move(rest, flip_y)
    xy_own, xy_one = move(x_own, flip_y), move(y_one, flip_x)
    xy_three, xy_two = move(x_rest[:rows], flip_y), move(y_rest[rows:], flip_x)
    parts = []
    for o, part in ((0, own), (2, x_own), (4, y_own), (6, xy_own)):
        parts.append((part, [(o, 0, 0, rows)]))
    for o, part in ((0, one), (2, x_one), (4, y_one), (6, xy_one)):
        parts.append((part, [(o, 1, 0, rows)]))
    for o, part in ((0, rest), (2, x_rest), (4, y_rest)):
        parts.append((part, [(o, 3, 0, rows), (o, 2, 0, rows)]))
    parts.append((xy_three, [(6, 3, 0, rows)]))
    parts.append((xy_two, [(6, 2, 0, rows)]))
    for part, where in list(parts):
        mirrored = [(o ^ 1, s, first, count) for o, s, first, count in where]
        parts.append((move(part, flip_core), mirrored))
    return [part for part, _ in parts], [where for _, where in parts], one


def prep_kernel(heads, len_ref, rate_ref, tok_ref, gain_ref, wg_ref, gate_ref, up_ref, down_ref, *refs):
    ffn_ref, normed_ref, weight_ref, carried_ref, tw_ref, decay_ref = refs[-6:]
    stripe = gate_ref.shape[0]
    if stripe % 128 == 0:
        ffn_ref[:, 0:stripe] = gate_ref[...].astype(F32).T.astype(BF16)
        ffn_ref[:, stripe : 2 * stripe] = up_ref[...].astype(F32).T.astype(BF16)
        ffn_ref[:, 2 * stripe :] = down_ref[...]
    else:
        ffn_ref[...] = jnp.zeros(ffn_ref.shape, BF16)
    requests = weight_ref.shape[0]
    rows = tok_ref.shape[0]
    length = rows // requests
    normed = rms_norm(tok_ref[...].astype(F32), gain_ref[...]).astype(BF16)
    normed_ref[...] = normed
    column = lax.broadcasted_iota(jnp.int32, (2 * heads, 256), 0)
    lane = lax.broadcasted_iota(jnp.int32, (2 * heads, 256), 1)
    chosen = (column == 2 * lane) | ((column == 2 * (lane - 128) + 1) & (lane >= 128))
    gates = jnp.dot(wg_ref[...], chosen.astype(F32).astype(BF16), preferred_element_type=F32)
    logits = jnp.dot(normed, gates.astype(BF16), preferred_element_type=F32)
    rate_lane = lax.broadcasted_iota(jnp.int32, (1, 128), 1)
    rate = jnp.zeros((1, 128), F32)
    for h in range(heads):
        rate = jnp.where(rate_lane == h, rate_ref[h], rate)
    position = lax.broadcasted_iota(jnp.int32, (length, 128), 0)
    lane = lax.broadcasted_iota(jnp.int32, (length, 128), 1)
    slot = jnp.where(lane < length, lane, lane - length)
    causal = position >= slot
    below = lax.broadcasted_iota(jnp.int32, (length, length), 0) >= lax.broadcasted_iota(
        jnp.int32, (length, length), 1
    )
    below = below.astype(F32)
    for r in range(requests):
        mine = logits[r * length : (r + 1) * length]
        live = (position < len_ref[r]).astype(F32)
        beta = jax.nn.sigmoid(mine[:, :128]) * live
        forget = mine[:, 128:]
        softplus = jnp.maximum(forget, 0.0) + jnp.log1p(jnp.exp(-jnp.abs(forget)))
        log_decay = -rate * softplus * live
        cum = jnp.dot(
            below, log_decay, precision=lax.Precision.HIGHEST, preferred_element_type=F32
        )
        last = cum[length - 1 : length]
        cum_rows = jnp.concatenate([cum, cum], axis=0).T
        beta_rows = jnp.concatenate([beta, beta], axis=0).T
        carried = jnp.exp(cum)
        tail_weight = jnp.exp(last - cum) * beta
        decay = jnp.exp(last)
        for h in range(heads):
            spread = cum[:, h : h + 1] - cum_rows[h : h + 1]
            weight = jnp.where(causal, jnp.exp(jnp.minimum(spread, 0.0)), 0.0)
            weight_ref[r, h] = weight * beta_rows[h : h + 1]
            carried_ref[r, h] = jnp.broadcast_to(carried[:, h : h + 1], (length, 128))
            tw_ref[r, h] = jnp.broadcast_to(tail_weight[:, h : h + 1], (length, 128))
            decay_ref[r, h : h + 1] = jnp.broadcast_to(decay[:, h : h + 1], (1, 128))


def prep_call(lengths, decay_rate, tokens, gain, w_gates, w_gate, w_up, w_down, behind):
    rows, width = tokens.shape
    requests, heads = lengths.shape[0], decay_rate.shape[0]
    length = rows // requests
    vmem = pl.BlockSpec(memory_space=pltpu.VMEM)
    smem = pl.BlockSpec(memory_space=pltpu.SMEM)
    wide = jax.ShapeDtypeStruct((requests, heads, length, 128), F32)
    return pl.pallas_call(
        functools.partial(prep_kernel, heads),
        in_specs=[smem] * 2 + [vmem] * 6 + [pl.BlockSpec(memory_space=pl.ANY)] * len(behind),
        out_specs=[vmem] * 6,
        out_shape=[
            jax.ShapeDtypeStruct((w_down.shape[0], 3 * w_down.shape[1]), BF16),
            jax.ShapeDtypeStruct((rows, width), BF16),
            wide,
            wide,
            wide,
            jax.ShapeDtypeStruct((requests, heads, 128), F32),
        ],
        compiler_params=pltpu.CompilerParams(vmem_limit_bytes=16 << 20),
        cost_estimate=cost(3 << 30, 1 << 16),
        name="norm_gates",
    )(lengths, decay_rate, tokens, gain.reshape(1, width), w_gates, w_gate, w_up, w_down, *in_hbm(behind))


def qkv_kernel(n_pieces, spans, chunk, at_ref, len_ref, x_ref, *refs):
    pieces = refs[:n_pieces]
    tail_ref, conv_ref = refs[n_pieces : n_pieces + 2]
    act_ref, new_tail_ref, weights, sems = refs[-4:]
    step = pl.program_id(0)
    columns = act_ref.shape[1]
    chunks = weights.shape[1] // chunk
    per_chunk = chunk // columns

    def copies(c):
        cut = pl.ds(c * chunk, chunk)
        for i, (piece, first, rows) in enumerate(spans):
            begin = pl.multiple_of(at_ref[i], 16)
            yield pltpu.make_async_copy(
                pieces[piece].at[pl.ds(first, rows), cut],
                weights.at[pl.ds(begin, rows), cut],
                sems.at[c, i],
            )

    @pl.when(step == 0)
    def _():
        for c in range(chunks):
            for copy in copies(c):
                copy.start()

    for c in range(chunks):

        @pl.when(step == c * per_chunk)
        def _():
            for copy in copies(c):
                copy.wait()

    mine = weights[:, pl.ds(pl.multiple_of(step * columns, columns), columns)]
    projected = jnp.dot(x_ref[...], mine, preferred_element_type=F32).astype(BF16)
    requests, window, _ = tail_ref.shape
    length = projected.shape[0] // requests
    is_vector = step < 4
    for r in range(requests):
        blank = jnp.zeros((TAIL_ROW, columns), F32)
        head_rows = jnp.concatenate([blank, tail_ref[r].astype(F32)], axis=0)
        mine = projected[r * length : (r + 1) * length].astype(F32)
        extended = jnp.concatenate([head_rows, mine], axis=0)
        wanted = lax.broadcasted_iota(jnp.int32, (8, extended.shape[0]), 0) + len_ref[r]
        place = lax.broadcasted_iota(jnp.int32, (8, extended.shape[0]), 1)
        chosen = (place == wanted + TAIL_ROW).astype(F32)
        rows = jnp.dot(chosen, extended, preferred_element_type=F32)
        new_tail_ref[r] = rows[:window].astype(BF16)
        total = conv_ref[0:1] * extended[TAIL_ROW : TAIL_ROW + length]
        for tap in range(1, window + 1):
            total = total + conv_ref[tap : tap + 1] * extended[
                TAIL_ROW + tap : TAIL_ROW + tap + length
            ]
        act = total * jax.nn.sigmoid(total)
        for h in range(columns // 128):
            head = act[:, h * 128 : (h + 1) * 128]
            scale = lax.rsqrt(jnp.sum(head * head, axis=-1, keepdims=True) + 1e-06)
            scale = jnp.where(is_vector, scale, jnp.ones_like(scale))
            act_ref[r * length : (r + 1) * length, h * 128 : (h + 1) * 128] = head * scale


def qkv_call(at, spans, lengths, x, pieces, tails, conv_weight, behind):
    rows, depth = x.shape
    columns = pieces[0].shape[1]
    requests, window = tails.shape[:2]
    wide, chunk = 512, 1024
    whole = lambda a: pl.BlockSpec(a.shape, lambda j, s, t: (0,) * a.ndim)
    tail_block = pl.BlockSpec((requests, window, wide), lambda j, s, t: (0, 0, j))
    return pl.pallas_call(
        functools.partial(qkv_kernel, len(pieces), spans, chunk),
        grid_spec=pltpu.PrefetchScalarGridSpec(
            num_scalar_prefetch=2,
            grid=(columns // wide,),
            in_specs=[whole(x)]
            + [pl.BlockSpec(memory_space=pltpu.HBM)] * len(pieces)
            + [tail_block, pl.BlockSpec((window + 1, wide), lambda j, s, t: (0, j))]
            + [pl.BlockSpec(memory_space=pl.ANY)] * len(behind),
            out_specs=[pl.BlockSpec((rows, wide), lambda j, s, t: (0, j)), tail_block],
            scratch_shapes=[
                pltpu.VMEM((depth, columns), BF16),
                pltpu.SemaphoreType.DMA((columns // chunk, len(spans))),
            ],
        ),
        out_shape=[
            jax.ShapeDtypeStruct((rows, columns), F32),
            jax.ShapeDtypeStruct(tails.shape, BF16),
        ],
        compiler_params=pltpu.CompilerParams(vmem_limit_bytes=24 << 20),
        cost_estimate=cost(5 << 30, 1 << 16),
        name="qkv_conv",
    )(at, lengths, x, *in_hbm(pieces), tails, conv_weight, *in_hbm(behind))


def stats_kernel(heads, place_ref, slot_ref, k_ref, v_ref, tw_ref, fd_ref, s_ref, vs_ref, tail_ref, out_ref):
    size = 128
    row = lax.broadcasted_iota(jnp.int32, (size, size), 0)
    col = lax.broadcasted_iota(jnp.int32, (size, size), 1)
    half = heads // 2
    contract = (((0,), (0,)), ((), ()))
    keys_end = []
    for h in range(heads):
        keys = k_ref[:, h * size : (h + 1) * size]
        values = v_ref[:, h * size : (h + 1) * size]
        tail_weight = tw_ref[0, h]
        both = jnp.concatenate([keys * tail_weight, values * tail_weight], axis=1).astype(BF16)
        sums = lax.dot_general(both, keys.astype(BF16), contract, preferred_element_type=F32)
        decay = fd_ref[0, h : h + 1]
        keys_end.append(decay * s_ref[0, h] + sums[:size])
        at = half * size + h * size
        out_ref[0, at : at + size] = (decay * vs_ref[0, h] + sums[size:]).astype(BF16)
    diagonals = []
    for p in range(half):
        low, high = keys_end[p], keys_end[p + half]
        out_ref[0, p * size : (p + 1) * size] = jnp.where(row >= col, low, high).astype(BF16)
        diagonals.append(jnp.sum(jnp.where(row == col, high, 0.0), axis=0, keepdims=True))
    at = (half + heads) * size
    slot = slot_ref[pl.program_id(0)].astype(F32)
    diagonals.append(jnp.full((16 - half, size), slot, F32))
    out_ref[0, at : at + 16] = jnp.concatenate(diagonals, axis=0).astype(BF16)
    tail = tail_ref[0].astype(F32)
    strips = [tail[:, c : c + size] for c in range(0, tail.shape[1], size)]
    fill = out_ref.shape[1] - at - 16 - len(strips) * tail.shape[0]
    strips.append(jnp.zeros((fill, size), F32))
    out_ref[0, at + 16 :] = jnp.concatenate(strips, axis=0).astype(BF16)


def stats_call(places, slots, act, tail_weight, decay, keys_start, values_start, tails):
    requests, heads = keys_start.shape[:2]
    length = act.shape[0] // requests
    width = heads * 128
    tail_rows = tails.shape[1] * tails.shape[2] // 128
    out_rows = (heads // 2 + heads) * 128 + 16 + tail_rows + -tail_rows % 16
    matrices = pl.BlockSpec((1, heads, 128, 128), lambda i, s, t: (i, 0, 0, 0))
    return pl.pallas_call(
        functools.partial(stats_kernel, heads),
        grid_spec=pltpu.PrefetchScalarGridSpec(
            num_scalar_prefetch=2,
            grid=(requests,),
            in_specs=[
                pl.BlockSpec((length, width), lambda i, s, t: (i, 1)),
                pl.BlockSpec((length, width), lambda i, s, t: (i, 2)),
                pl.BlockSpec((1, heads, length, 128), lambda i, s, t: (i, 0, 0, 0)),
                pl.BlockSpec((1, heads, 128), lambda i, s, t: (i, 0, 0)),
                matrices,
                matrices,
                pl.BlockSpec((1,) + tails.shape[1:], lambda i, s, t: (i, 0, 0)),
            ],
            out_specs=pl.BlockSpec((1, out_rows, 128), lambda i, s, t: (s[i], 0, 0)),
        ),
        out_shape=jax.ShapeDtypeStruct((requests, out_rows, 128), BF16),
        compiler_params=pltpu.CompilerParams(vmem_limit_bytes=16 << 20),
        cost_estimate=cost(3 << 30, 1 << 16),
        name="stats",
    )(places, slots, act, act, tail_weight, decay, *in_hbm([keys_start, values_start]), tails)


def unpack_kernel(heads, part_ref, keys_ref, values_ref, tail_ref, keys_buf, values_buf, tail_buf, sems):
    size = 128
    half = heads // 2
    window, columns = tail_ref.shape[1:]
    row = lax.broadcasted_iota(jnp.int32, (size, size), 0)
    col = lax.broadcasted_iota(jnp.int32, (size, size), 1)
    n_parts = part_ref.shape[0]
    under_way = []
    for s in range(n_parts):
        buf = s % 2
        if s >= 2:
            for copy in under_way[s - 2]:
                copy.wait()
        at = (half + heads) * size
        diagonals = part_ref[s, at : at + 16].astype(F32)
        slot = jnp.max(diagonals[half : half + 1]).astype(jnp.int32)
        for p in range(half):
            packed = part_ref[s, p * size : (p + 1) * size].astype(F32)
            turned = packed.T
            keys_buf[buf, p] = jnp.where(row >= col, packed, turned)
            keys_buf[buf, p + half] = jnp.where(
                row < col, packed, jnp.where(row == col, diagonals[p : p + 1], turned)
            )
        for h in range(heads):
            begin = (half + h) * size
            values_buf[buf, h] = part_ref[s, begin : begin + size].astype(F32)
        rows = part_ref[s, at + 16 :].astype(F32)
        strips = [rows[c * window : (c + 1) * window] for c in range(columns // size)]
        tail_buf[s] = jnp.concatenate(strips, axis=1).astype(BF16)
        copies = [
            pltpu.make_async_copy(keys_buf.at[buf], keys_ref.at[slot], sems.at[s, 0]),
            pltpu.make_async_copy(values_buf.at[buf], values_ref.at[slot], sems.at[s, 1]),
            pltpu.make_async_copy(tail_buf.at[s], tail_ref.at[slot], sems.at[s, 2]),
        ]
        for copy in copies:
            copy.start()
        under_way.append(copies)
    for copies in under_way[-2:]:
        for copy in copies:
            copy.wait()


def unpack_call(parts, heads, tail_shape):
    n_parts = parts.shape[0]
    vmem = pl.BlockSpec(memory_space=pltpu.VMEM)
    hbm = pl.BlockSpec(memory_space=pltpu.HBM)
    matrices = jax.ShapeDtypeStruct((n_parts, heads, 128, 128), F32)
    return pl.pallas_call(
        functools.partial(unpack_kernel, heads),
        in_specs=[vmem],
        out_specs=[hbm, hbm, hbm],
        out_shape=[matrices, matrices, jax.ShapeDtypeStruct((n_parts,) + tail_shape, BF16)],
        scratch_shapes=[
            pltpu.VMEM((2, heads, 128, 128), F32),
            pltpu.VMEM((2, heads, 128, 128), F32),
            pltpu.VMEM((n_parts,) + tail_shape, BF16),
            pltpu.SemaphoreType.DMA((n_parts, 3)),
        ],
        compiler_params=pltpu.CompilerParams(vmem_limit_bytes=16 << 20),
        cost_estimate=cost(3 << 30, 1 << 16),
        name="unpack",
    )(parts)


def two_terms(values):
    high = values.astype(BF16)
    low = (values - high.astype(F32)).astype(BF16)
    return high, low


def lane_sum(values):
    return jnp.sum(values, axis=-1, keepdims=True)


def cg_kernel(heads, group, ridge_ref, q_ref, k_ref, v_ref, w_ref, c_ref, s_ref, vs_ref, *refs):
    out_ref = refs[-1]
    size = 128
    first_half = lax.broadcasted_iota(jnp.int32, (q_ref.shape[0], size), 1) < size // 2
    transposed = (((1,), (1,)), ((), ()))
    for base in range(0, heads, group):
        hs = range(base, base + group)
        keys = [k_ref[:, h * size : (h + 1) * size] for h in hs]
        keys2 = [jnp.concatenate([k, k], axis=0) for k in keys]
        keys2_bf = [k.astype(BF16) for k in keys2]
        keys_t = [k.T.astype(BF16) for k in keys2]
        system = []
        for i, h in enumerate(hs):
            m = jnp.concatenate([s_ref[0, h].astype(BF16), keys_t[i]], axis=1)
            system.append(jnp.concatenate([m, m], axis=0))

        def both_terms(field):
            return jnp.concatenate(two_terms(field), axis=1)

        def scored(products, i, h):
            scores = products[:, size:] * w_ref[0, h]
            high = scores.astype(BF16).astype(F32)
            return jnp.where(first_half, high, scores - high).astype(BF16)

        direction = [q_ref[:, h * size : (h + 1) * size] for h in hs]
        residual = list(direction)
        total = [None] * group
        norm = [lane_sum(r * r) for r in residual]
        for it in range(ITERS):
            products = [
                jnp.dot(both_terms(direction[i]), system[i], preferred_element_type=F32)
                for i in range(group)
            ]
            spread = [
                jnp.dot(scored(products[i], i, h), keys2_bf[i], preferred_element_type=F32)
                for i, h in enumerate(hs)
            ]
            for i, h in enumerate(hs):
                applied = (
                    c_ref[0, h] * products[i][:, :size] + spread[i] + ridge_ref[h] * direction[i]
                )
                step = norm[i] / (lane_sum(direction[i] * applied) + 1e-20)
                moved = step * direction[i]
                total[i] = moved if total[i] is None else total[i] + moved
                if it + 1 < ITERS:
                    residual[i] = residual[i] - step * applied
                    following = lane_sum(residual[i] * residual[i])
                    direction[i] = residual[i] + following / (norm[i] + 1e-20) * direction[i]
                    norm[i] = following
        for i, h in enumerate(hs):
            start_m = jnp.concatenate([vs_ref[0, h].astype(BF16), keys2_bf[i]], axis=0)
            start_m = jnp.concatenate([start_m, start_m], axis=1)
            products = lax.dot_general(
                both_terms(total[i]), start_m, transposed, preferred_element_type=F32
            )
            values = v_ref[:, h * size : (h + 1) * size]
            values2 = jnp.concatenate([values, values], axis=0).astype(BF16)
            read = c_ref[0, h] * products[:, :size] + jnp.dot(
                scored(products, i, h), values2, preferred_element_type=F32
            )
            out_ref[:, h * size : (h + 1) * size] = read.astype(BF16)


def cg_call(ridge, act, weight2, carried, keys_start, values_start, first, count, behind):
    requests, heads = keys_start.shape[:2]
    length = act.shape[0] // requests
    width = heads * 128
    per_head = lambda rows: pl.BlockSpec((1, heads, rows, 128), lambda i: (i + first, 0, 0, 0))
    return pl.pallas_call(
        functools.partial(cg_kernel, heads, 4),
        grid=(count,),
        in_specs=[
            pl.BlockSpec(memory_space=pltpu.SMEM),
            pl.BlockSpec((length, width), lambda i: (i + first, 0)),
            pl.BlockSpec((length, width), lambda i: (i + first, 1)),
            pl.BlockSpec((length, width), lambda i: (i + first, 2)),
            per_head(length),
            per_head(length),
            per_head(128),
            per_head(128),
        ]
        + [pl.BlockSpec(memory_space=pl.ANY)] * len(behind),
        out_specs=pl.BlockSpec((length, width), lambda i: (i, 0)),
        out_shape=jax.ShapeDtypeStruct((count * length, width), BF16),
        compiler_params=pltpu.CompilerParams(vmem_limit_bytes=20 << 20),
        cost_estimate=cost(4 << 30, 1 << 16),
        name="cg",
    )(ridge, act, act, act, weight2, carried, *in_hbm([keys_start, values_start]), *in_hbm(behind))


def out_kernel(x_ref, tok_ref, gain_ref, w_ref, *refs):
    after_ref, in_ref = refs[-2:]
    attended = jnp.dot(x_ref[...], w_ref[...], preferred_element_type=F32)
    after_attn = (tok_ref[...].astype(F32) + attended).astype(BF16)
    after_ref[...] = after_attn
    in_ref[...] = rms_norm(after_attn.astype(F32), gain_ref[...]).astype(BF16)


def out_call(head_rows, tokens, first, gain, weights, behind):
    rows, width = head_rows.shape[0], tokens.shape[1]
    whole = lambda a: pl.BlockSpec(a.shape, lambda i: (0, 0))
    return pl.pallas_call(
        out_kernel,
        grid=(1,),
        in_specs=[
            whole(head_rows),
            pl.BlockSpec((rows, width), lambda i: (first, 0)),
            whole(gain),
            whole(weights),
        ]
        + [pl.BlockSpec(memory_space=pl.ANY)] * len(behind),
        out_specs=[pl.BlockSpec((rows, width), lambda i: (0, 0))] * 2,
        out_shape=[jax.ShapeDtypeStruct((rows, width), BF16)] * 2,
        compiler_params=pltpu.CompilerParams(vmem_limit_bytes=16 << 20),
        cost_estimate=cost(2 << 30, 1 << 16),
        name="out_proj",
    )(head_rows, tokens, gain, weights, *in_hbm(behind))


def ffn_kernel(spans, blocks, counts, order_ref, *refs):
    n_in, n_out = counts
    inputs, pieces = refs[:n_in], refs[n_in : -4 - n_out]
    outputs = refs[-4 - n_out : -4]
    gate_w, up_w, down_w, sems = refs[-4:]
    size = 128
    matrices = (gate_w, up_w, down_w)

    def copies(block, which):
        for i, (piece, first, j) in enumerate(spans[block]):
            to = pl.ds(pl.multiple_of(order_ref[j] * size, size), size)
            yield pltpu.make_async_copy(
                pieces[piece].at[pl.ds(first, gate_w.shape[1]), pl.ds(which * size, size)],
                matrices[which].at[block, :, to],
                sems.at[block, which, i],
            )

    for block in range(blocks):
        for which in range(3):
            for copy in copies(block, which):
                copy.start()
    x = jnp.concatenate([ref[...] for ref in inputs], axis=0)
    turned = (((1,), (1,)), ((), ()))
    total = None
    for block in range(blocks):
        for copy in copies(block, 0):
            copy.wait()
        gate = lax.dot_general(x, gate_w[block], turned, preferred_element_type=F32)
        for copy in copies(block, 1):
            copy.wait()
        up = lax.dot_general(x, up_w[block], turned, preferred_element_type=F32)
        hidden = (gate * jax.nn.sigmoid(gate) * up).astype(BF16)
        for copy in copies(block, 2):
            copy.wait()
        sums = jnp.dot(hidden, down_w[block], preferred_element_type=F32)
        total = sums if total is None else total + sums
    begin = 0
    for out_ref in outputs:
        rows = out_ref.shape[0]
        out_ref[...] = total[begin : begin + rows].astype(out_ref.dtype)
        begin += rows


def ffn_call(order, spans, inputs, pieces, outputs, behind):
    width = inputs[0].shape[1]
    blocks = len(spans)
    hidden = pieces[0].shape[0]
    vmem = pl.BlockSpec(memory_space=pltpu.VMEM)
    matrix = pltpu.VMEM((blocks, hidden, width), BF16)
    return pl.pallas_call(
        functools.partial(ffn_kernel, spans, blocks, (len(inputs), len(outputs))),
        grid_spec=pltpu.PrefetchScalarGridSpec(
            num_scalar_prefetch=1,
            grid=(),
            in_specs=[vmem] * len(inputs)
            + [pl.BlockSpec(memory_space=pltpu.HBM)] * len(pieces)
            + [pl.BlockSpec(memory_space=pl.ANY)] * len(behind),
            out_specs=[vmem] * len(outputs),
            scratch_shapes=[
                matrix,
                matrix,
                matrix,
                pltpu.SemaphoreType.DMA((blocks, 3, len(spans[0]))),
            ],
        ),
        out_shape=[jax.ShapeDtypeStruct((rows, width), kind) for rows, kind in outputs],
        compiler_params=pltpu.CompilerParams(vmem_limit_bytes=32 << 20),
        cost_estimate=cost(5 << 30, 1 << 16),
        name="ffn",
    )(order, *inputs, *in_hbm(pieces), *in_hbm(behind))


def shards(
    tokens,
    lengths,
    ridge_keys,
    ridge_values,
    conv_tail,
    page_table,
    w_qkv,
    conv_weight,
    w_gates,
    decay_rate,
    ridge,
    w_out,
    attn_gain,
    ffn_gain,
    w_gate,
    w_up,
    w_down,
):
    requests, length, width = tokens.shape
    heads = decay_rate.shape[0]
    row_count = requests * length
    reqs, peers = lax.axis_size("req"), lax.axis_size("mesh")
    my_req, my_mesh = lax.axis_index("req"), lax.axis_index("mesh")
    move = lambda value, pairs: lax.ppermute(value, AXES, pairs)
    hop_one, hop_two = flip_mesh(1, reqs, peers), flip_mesh(2, reqs, peers)
    own_rows = w_qkv.shape[0]

    w_out_all = lax.all_gather(w_out, AXES, axis=0, tiled=True)
    flat_tokens = tokens.reshape(row_count, width)
    prep = functools.partial(
        prep_call, lengths, decay_rate, flat_tokens, attn_gain, w_gates, w_gate, w_up, w_down
    )
    if (reqs, peers) == (8, 4):
        shifts = {s: shift_mesh(s, reqs, peers) for s in range(1, peers)}
        flips = [flip_req(bit, reqs, peers) for bit in (1, 2, 4)]
        qkv_pieces, places, early = gather_rows(w_qkv, move, shifts, flips)
        spans = []
        for piece, listed in enumerate(places):
            begin = 0
            for _, _, _, count in listed:
                spans.append((piece, begin, count))
                begin += count
        listed = np.array([place for part in places for place in part], np.int32)
        owner = (my_req ^ listed[:, 0]) * peers + (my_mesh - listed[:, 1]) % peers
        qkv_at = owner * own_rows + listed[:, 2]
        ffn_own, normed, weight2, carried, tail_weight, decay = prep([early])
        ffn_two = move(ffn_own, hop_two)
        x_own, y_own = move(ffn_own, flips[1]), move(ffn_own, flips[2])
        x_two, y_two = move(ffn_two, flips[1]), move(ffn_two, flips[2])
        xy_own, xy_two = move(x_own, flips[2]), move(y_two, flips[1])
        ffn_pieces = [ffn_own, x_own, y_own, xy_own, ffn_two, x_two, y_two, xy_two]
        ffn_pieces = ffn_pieces + [move(p, flips[0]) for p in ffn_pieces]
        ffn_order = my_req ^ np.array((0, 2, 4, 6, 1, 3, 5, 7), np.int32)
        ffn_spans = [
            [(4 * i + j, 0, j) for j in range(4)] + [(8 + 4 * i + j, 0, 4 + j) for j in range(4)]
            for i in (0, 1)
        ]
        behind_qkv, behind_a = [ffn_two], [x_own, y_own]
        behind_b, behind_out = [x_two, y_two, xy_own], [xy_two]
    else:
        w_qkv_all = lax.all_gather(w_qkv, AXES, axis=0, tiled=True)
        qkv_pieces = [w_qkv_all]
        spans = [(0, 0, w_qkv_all.shape[0])]
        qkv_at = jnp.zeros((1,), jnp.int32)
        _, normed, weight2, carried, tail_weight, decay = prep([])
        gate_all = lax.all_gather(w_gate, "req", axis=0, tiled=True)
        up_all = lax.all_gather(w_up, "req", axis=0, tiled=True)
        down_all = lax.all_gather(w_down, "req", axis=1, tiled=True)
        stripes = width // 128
        ffn_pieces = []
        for j in range(stripes):
            cut = slice(j * 128, (j + 1) * 128)
            piece = jnp.concatenate([gate_all[cut].T, up_all[cut].T, down_all[:, cut]], axis=1)
            ffn_pieces.append(piece)
        ffn_pieces = ffn_pieces + [move(piece, hop_two) for piece in ffn_pieces]
        ffn_spans = [[(i * stripes + j, 0, j) for j in range(stripes)] for i in (0, 1)]
        ffn_order = jnp.arange(stripes)
        behind_qkv, behind_a, behind_b, behind_out = [], [], [], []
    ffn_order = ffn_order.astype(jnp.int32)

    act, new_tail = qkv_call(
        qkv_at.astype(jnp.int32), spans, lengths, normed, qkv_pieces, conv_tail, conv_weight,
        behind_qkv,
    )

    packed = stats_call(
        page_table // requests,
        page_table % requests,
        act,
        tail_weight,
        decay,
        ridge_keys,
        ridge_values,
        new_tail,
    )
    parts = lax.all_to_all(packed, "mesh", split_axis=0, concat_axis=0, tiled=True)
    keys_decode, values_decode, tail_decode = unpack_call(parts, heads, conv_tail.shape[1:])

    per = requests // 2
    part_rows = per * length
    gain = ffn_gain.reshape(1, width)
    system = (ridge, act, weight2, carried, ridge_keys, ridge_values)
    heads_a = cg_call(*system, 0, per, [packed] + behind_a)
    after_a, in_a = out_call(heads_a, flat_tokens, 0, gain, w_out_all, [])
    theirs_a = move(in_a, hop_one)
    heads_b = cg_call(*system, per, per, [in_a] + behind_b)
    after_b, in_b = out_call(heads_b, flat_tokens, 1, gain, w_out_all, behind_out)
    theirs_b = move(in_b, hop_one)
    mine_a, mine_b, for_a = ffn_call(
        ffn_order,
        ffn_spans,
        [in_a, in_b, theirs_a],
        ffn_pieces,
        [(part_rows, F32), (part_rows, F32), (part_rows, BF16)],
        [],
    )
    got_a = move(for_a, hop_one)
    (for_b,) = ffn_call(
        ffn_order, ffn_spans, [theirs_b], ffn_pieces, [(part_rows, BF16)], [for_a]
    )
    got_b = move(for_b, hop_one)
    mixed = [
        (after_attn.astype(F32) + (mine + got.astype(F32))).astype(BF16)
        for after_attn, mine, got in ((after_a, mine_a, got_a), (after_b, mine_b, got_b))
    ]
    return (
        jnp.concatenate(mixed, axis=0).reshape(requests, length, width),
        keys_decode,
        values_decode,
        tail_decode,
        jnp.concatenate([heads_a, heads_b], axis=0).reshape(requests, length, -1),
    )


def solution(mesh):
    rows = P(AXES)
    in_specs = (
        rows,
        rows,
        rows,
        rows,
        rows,
        rows,
        rows,
        P(),
        P(),
        P(),
        P(),
        rows,
        P(),
        P(),
        P("req", "mesh"),
        P("req", "mesh"),
        P("mesh", "req"),
    )
    out_specs = (rows, rows, rows, rows, rows)
    return jax.shard_map(shards, mesh=mesh, in_specs=in_specs, out_specs=out_specs, check_vma=False)
```

```python
import functools

import jax
import jax.numpy as jnp
import numpy as np
from jax import lax
from jax.experimental import pallas as pl
from jax.experimental.pallas import tpu as pltpu
from jax.sharding import PartitionSpec as P

ITERS = 5
AXES = ("req", "mesh")
TAIL_ROW = 5
F32 = jnp.float32
BF16 = jnp.bfloat16


def rms_norm(values, gain):
    return values * lax.rsqrt(jnp.mean(values * values, axis=-1, keepdims=True) + 1e-05) * gain


def cost(flops, bytes_accessed):
    return pl.CostEstimate(flops=flops, bytes_accessed=bytes_accessed, transcendentals=0)


def in_hbm(values):
    return [pltpu.with_memory_space_constraint(value, pltpu.HBM) for value in values]


def in_vmem(values):
    return [pltpu.with_memory_space_constraint(value, pltpu.VMEM) for value in values]


def flip_req(bit, reqs, peers):
    return [(r * peers + z, (r ^ bit) * peers + z) for r in range(reqs) for z in range(peers)]


def shift_mesh(step, reqs, peers):
    return [(r * peers + z, r * peers + (z + step) % peers) for r in range(reqs) for z in range(peers)]


def flip_mesh(bit, reqs, peers):
    return [(r * peers + z, r * peers + (z ^ bit)) for r in range(reqs) for z in range(peers)]


def gather_rows(own, move, shifts, flips, beside):
    flip_x, flip_y = flips
    rows = own.shape[0]
    one = move(own, shifts[1])
    x_own, y_own = move(own, flip_x), move(own, flip_y)
    three = move(own, shifts[3])
    two = move(one, shifts[1])
    x_one, y_one = move(one, flip_x), move(one, flip_y)
    *results, three = beside(three, [x_own, y_own])
    (two,) = release_call([two], [x_one, y_one])
    rest = jnp.concatenate([three, two], axis=0)
    x_rest, y_rest = move(rest, flip_x), move(rest, flip_y)
    xy_own, xy_one = move(x_own, flip_y), move(y_one, flip_x)
    xy_three, xy_two = move(x_rest[:rows], flip_y), move(y_rest[rows:], flip_x)
    parts = []
    for o, part in ((0, own), (2, x_own), (4, y_own), (6, xy_own)):
        parts.append((part, [(o, 0)]))
    for o, part in ((0, one), (2, x_one), (4, y_one), (6, xy_one)):
        parts.append((part, [(o, 1)]))
    for o, part in ((0, rest), (2, x_rest), (4, y_rest)):
        parts.append((part, [(o, 3), (o, 2)]))
    parts.append((xy_three, [(6, 3)]))
    parts.append((xy_two, [(6, 2)]))
    return [part for part, _ in parts], [where for _, where in parts], results, two, [xy_three, xy_two]


def prep_kernel(heads, len_ref, rate_ref, tok_ref, gain_ref, wg_ref, *refs):
    gate_ref, up_ref, down_ref = refs[:3]
    ffn_ref, normed_ref, weight_ref, carried_ref, tw_ref, decay_ref = refs[-7:-1]
    stripe = down_ref.shape[1]
    if stripe % 128 == 0:
        ffn_ref[:, 0:stripe] = gate_ref[...]
        ffn_ref[:, stripe : 2 * stripe] = up_ref[...]
        ffn_ref[:, 2 * stripe :] = down_ref[...]
    else:
        ffn_ref[...] = jnp.zeros(ffn_ref.shape, BF16)
    requests = weight_ref.shape[0]
    rows = tok_ref.shape[0]
    length = rows // requests
    normed = rms_norm(tok_ref[...].astype(F32), gain_ref[...]).astype(BF16)
    normed_ref[...] = normed
    lane = lax.broadcasted_iota(jnp.int32, (256, 2 * heads), 0)
    column = lax.broadcasted_iota(jnp.int32, (256, 2 * heads), 1)
    chosen = (column == 2 * lane) | ((column == 2 * (lane - 128) + 1) & (lane >= 128))
    gates = jnp.dot(chosen.astype(F32).astype(BF16), wg_ref[...], preferred_element_type=F32)
    logits = lax.dot_general(
        normed, gates.astype(BF16), (((1,), (1,)), ((), ())), preferred_element_type=F32
    )
    rate_lane = lax.broadcasted_iota(jnp.int32, (1, 128), 1)
    rate = jnp.zeros((1, 128), F32)
    for h in range(heads):
        rate = jnp.where(rate_lane == h, rate_ref[h], rate)
    position = lax.broadcasted_iota(jnp.int32, (length, 128), 0)
    lane = lax.broadcasted_iota(jnp.int32, (length, 128), 1)
    slot = jnp.where(lane < length, lane, lane - length)
    causal = position >= slot
    below = lax.broadcasted_iota(jnp.int32, (length, length), 0) >= lax.broadcasted_iota(
        jnp.int32, (length, length), 1
    )
    below = below.astype(F32)
    for r in range(requests):
        mine = logits[r * length : (r + 1) * length]
        live = (position < len_ref[r]).astype(F32)
        beta = jax.nn.sigmoid(mine[:, :128]) * live
        forget = mine[:, 128:]
        softplus = jnp.maximum(forget, 0.0) + jnp.log1p(jnp.exp(-jnp.abs(forget)))
        log_decay = -rate * softplus * live
        cum = jnp.dot(
            below, log_decay, precision=lax.Precision.HIGHEST, preferred_element_type=F32
        )
        last = cum[length - 1 : length]
        cum_rows = jnp.concatenate([cum, cum], axis=0).T
        beta_rows = jnp.concatenate([beta, beta], axis=0).T
        carried = jnp.exp(cum)
        tail_weight = jnp.exp(last - cum) * beta
        decay = jnp.exp(last)
        for h in range(heads):
            spread = cum[:, h : h + 1] - cum_rows[h : h + 1]
            weight = jnp.where(causal, jnp.exp(jnp.minimum(spread, 0.0)), 0.0)
            weight_ref[r, h] = weight * beta_rows[h : h + 1]
            carried_ref[r, h] = jnp.broadcast_to(carried[:, h : h + 1], (length, 128))
            tw_ref[r, h] = jnp.broadcast_to(tail_weight[:, h : h + 1], (length, 128))
            decay_ref[r, h : h + 1] = jnp.broadcast_to(decay[:, h : h + 1], (1, 128))


def prep_call(lengths, decay_rate, tokens, gain, w_gates, ffn_weights, through, behind):
    rows, width = tokens.shape
    requests, heads = lengths.shape[0], decay_rate.shape[0]
    length = rows // requests
    smem = pl.BlockSpec(memory_space=pltpu.SMEM)
    hbm = pl.BlockSpec(memory_space=pltpu.HBM)
    whole = lambda shape: pl.BlockSpec(shape, lambda i: (0,) * len(shape))
    inputs = [tokens, gain.reshape(1, width), w_gates.T, *ffn_weights]
    hidden, stripe = ffn_weights[0].shape
    wide = (requests, heads, length, 128)
    shapes = [(hidden, 3 * stripe), (rows, width), wide, wide, wide, (requests, heads, 128)]
    return pl.pallas_call(
        functools.partial(prep_kernel, heads),
        grid=(1,),
        in_specs=[smem] * 2 + [whole(value.shape) for value in inputs] + [hbm] * (1 + len(behind)),
        out_specs=[whole(shape) for shape in shapes] + [hbm],
        out_shape=[pltpu.HBM(shape, F32 if i > 1 else BF16) for i, shape in enumerate(shapes)]
        + [pltpu.HBM(through.shape, through.dtype)],
        input_output_aliases={2 + len(inputs): len(shapes)},
        compiler_params=pltpu.CompilerParams(vmem_limit_bytes=20 << 20),
        cost_estimate=cost(3 << 30, 1 << 16),
        name="norm_gates",
    )(lengths, decay_rate, *in_hbm(inputs + [through] + behind))


def split_kernel(core_ref, w_ref, keep_ref, send_ref):
    wide = keep_ref.shape[1] // 3
    for which in range(3):
        to = slice(which * wide, (which + 1) * wide)
        for out_ref, half in ((keep_ref, core_ref[0]), (send_ref, 1 - core_ref[0])):
            begin = pl.multiple_of((2 * which + half) * wide, wide)
            out_ref[:, to] = w_ref[:, pl.ds(begin, wide)]


def split_call(core, weights):
    rows, columns = weights.shape
    vmem = pl.BlockSpec(memory_space=pltpu.VMEM)
    return pl.pallas_call(
        split_kernel,
        in_specs=[pl.BlockSpec(memory_space=pltpu.SMEM), vmem],
        out_specs=[vmem] * 2,
        out_shape=[jax.ShapeDtypeStruct((rows, columns // 2), BF16)] * 2,
        cost_estimate=cost(1 << 28, 1 << 16),
        name="split_heads",
    )(core, weights)


def project_kernel(n_pieces, spans, at_ref, x_ref, other_ref, *refs):
    pieces = refs[:n_pieces]
    mine_ref, theirs_ref, weights, sems = refs[-4:]
    step = pl.program_id(0)
    columns = mine_ref.shape[1]
    chunks = weights.shape[1] // columns

    def copies(c):
        cut = pl.ds(c * columns, columns)
        for i, (piece, first, rows) in enumerate(spans):
            begin = pl.multiple_of(at_ref[i], 16)
            yield pltpu.make_async_copy(
                pieces[piece].at[pl.ds(first, rows), cut],
                weights.at[pl.ds(begin, rows), cut],
                sems.at[c, i],
            )

    @pl.when(step == 0)
    def _():
        for c in range(chunks):
            for copy in copies(c):
                copy.start()

    for c in range(chunks):

        @pl.when(step == c)
        def _():
            for copy in copies(c):
                copy.wait()

    now = weights[:, pl.ds(pl.multiple_of(step * columns, columns), columns)]
    theirs = jnp.dot(other_ref[...], now, preferred_element_type=F32)
    theirs_ref[...] = theirs.astype(BF16)
    mine_ref[...] = jnp.dot(x_ref[...], now, preferred_element_type=F32).astype(BF16)


def project_call(at, spans, x, other, pieces, behind):
    rows, depth = x.shape
    columns = pieces[0].shape[1]
    wide = 512
    whole = pl.BlockSpec(x.shape, lambda j, s: (0, 0))
    block = pl.BlockSpec((rows, wide), lambda j, s: (0, j))
    return pl.pallas_call(
        functools.partial(project_kernel, len(pieces), spans),
        grid_spec=pltpu.PrefetchScalarGridSpec(
            num_scalar_prefetch=1,
            grid=(columns // wide,),
            in_specs=[whole, whole] + [pl.BlockSpec(memory_space=pltpu.HBM)] * len(pieces + behind),
            out_specs=[block, block],
            scratch_shapes=[
                pltpu.VMEM((depth, columns), BF16),
                pltpu.SemaphoreType.DMA((columns // wide, len(spans))),
            ],
        ),
        out_shape=[pltpu.HBM((rows, columns), BF16)] * 2,
        compiler_params=pltpu.CompilerParams(vmem_limit_bytes=16 << 20),
        cost_estimate=cost(3 << 30, 1 << 16),
        name="project",
    )(at, *in_hbm([x, other] + pieces + behind))


def conv_kernel(half_ref, len_ref, projected_ref, tail_ref, conv_ref, *refs):
    act_ref, new_tail_ref = refs[-2:]
    requests, window, columns = tail_ref.shape
    length = projected_ref.shape[0] // requests
    is_vector = pl.program_id(0) < 2
    for r in range(requests):
        blank = jnp.zeros((TAIL_ROW, columns), F32)
        head_rows = jnp.concatenate([blank, tail_ref[r].astype(F32)], axis=0)
        mine = projected_ref[r * length : (r + 1) * length].astype(F32)
        extended = jnp.concatenate([head_rows, mine], axis=0)
        wanted = lax.broadcasted_iota(jnp.int32, (8, extended.shape[0]), 0) + len_ref[r]
        place = lax.broadcasted_iota(jnp.int32, (8, extended.shape[0]), 1)
        chosen = (place == wanted + TAIL_ROW).astype(F32)
        rows = jnp.dot(chosen, extended, preferred_element_type=F32)
        new_tail_ref[r] = rows[:window].astype(BF16)
        total = conv_ref[0:1] * extended[TAIL_ROW : TAIL_ROW + length]
        for tap in range(1, window + 1):
            total = total + conv_ref[tap : tap + 1] * extended[
                TAIL_ROW + tap : TAIL_ROW + tap + length
            ]
        act = total * jax.nn.sigmoid(total)
        for h in range(columns // 128):
            head = act[:, h * 128 : (h + 1) * 128]
            scale = lax.rsqrt(jnp.sum(head * head, axis=-1, keepdims=True) + 1e-06)
            scale = jnp.where(is_vector, scale, jnp.ones_like(scale))
            act_ref[r * length : (r + 1) * length, h * 128 : (h + 1) * 128] = head * scale


def conv_call(half, lengths, projected, tails, conv_weight, held):
    rows, columns = projected.shape
    requests, window = tails.shape[:2]
    wide = columns // 3
    rows_block = pl.BlockSpec((rows, wide), lambda j, s, t: (0, 2 * j + s[0]))
    tail_block = pl.BlockSpec((requests, window, wide), lambda j, s, t: (0, 0, 2 * j + s[0]))
    return pl.pallas_call(
        conv_kernel,
        grid_spec=pltpu.PrefetchScalarGridSpec(
            num_scalar_prefetch=2,
            grid=(3,),
            in_specs=[
                pl.BlockSpec((rows, wide), lambda j, s, t: (0, j)),
                tail_block,
                pl.BlockSpec((window + 1, wide), lambda j, s, t: (0, 2 * j + s[0])),
            ]
            + [pl.BlockSpec(memory_space=pl.ANY)] * len(held),
            out_specs=[rows_block, tail_block],
        ),
        out_shape=[
            pltpu.HBM((rows, 2 * columns), F32),
            pltpu.HBM(tails.shape, BF16),
        ],
        input_output_aliases={5: 0, 6: 1} if held else {},
        compiler_params=pltpu.CompilerParams(vmem_limit_bytes=16 << 20),
        cost_estimate=cost(2 << 30, 1 << 16),
        name="conv_norm",
    )(half, lengths, *in_hbm([projected, tails, conv_weight] + held))


def stats_kernel(heads, place_ref, slot_ref, k_ref, v_ref, tw_ref, fd_ref, s_ref, vs_ref, *refs):
    tail_ref, out_ref = refs
    size = 128
    row = lax.broadcasted_iota(jnp.int32, (size, size), 0)
    col = lax.broadcasted_iota(jnp.int32, (size, size), 1)
    half = heads // 2
    contract = (((0,), (0,)), ((), ()))
    keys_end = []
    for h in range(heads):
        keys = k_ref[:, h * size : (h + 1) * size]
        values = v_ref[:, h * size : (h + 1) * size]
        tail_weight = tw_ref[0, h]
        both = jnp.concatenate([keys * tail_weight, values * tail_weight], axis=1).astype(BF16)
        sums = lax.dot_general(both, keys.astype(BF16), contract, preferred_element_type=F32)
        decay = fd_ref[0, h : h + 1]
        keys_end.append(decay * s_ref[0, h] + sums[:size])
        at = half * size + h * size
        out_ref[0, at : at + size] = (decay * vs_ref[0, h] + sums[size:]).astype(BF16)
    diagonals = []
    for p in range(half):
        low, high = keys_end[p], keys_end[p + half]
        out_ref[0, p * size : (p + 1) * size] = jnp.where(row >= col, low, high).astype(BF16)
        diagonals.append(jnp.sum(jnp.where(row == col, high, 0.0), axis=0, keepdims=True))
    at = (half + heads) * size
    slot = slot_ref[pl.program_id(0)].astype(F32)
    diagonals.append(jnp.full((16 - half, size), slot, F32))
    out_ref[0, at : at + 16] = jnp.concatenate(diagonals, axis=0).astype(BF16)
    tail = tail_ref[0].astype(F32)
    strips = [tail[:, c : c + size] for c in range(0, tail.shape[1], size)]
    fill = out_ref.shape[1] - at - 16 - len(strips) * tail.shape[0]
    strips.append(jnp.zeros((fill, size), F32))
    out_ref[0, at + 16 :] = jnp.concatenate(strips, axis=0).astype(BF16)


def stats_call(places, slots, act, tail_weight, decay, keys_start, values_start, tails):
    requests, heads = keys_start.shape[:2]
    length, width = act.shape[0] // requests, heads * 128
    tail_rows = tails.shape[1] * tails.shape[2] // 128
    out_rows = (heads // 2 + heads) * 128 + 16 + tail_rows + -tail_rows % 16
    matrices = pl.BlockSpec((1, heads, 128, 128), lambda i, s, t: (i, 0, 0, 0))
    return pl.pallas_call(
        functools.partial(stats_kernel, heads),
        grid_spec=pltpu.PrefetchScalarGridSpec(
            num_scalar_prefetch=2,
            grid=(requests,),
            in_specs=[
                pl.BlockSpec((length, width), lambda i, s, t: (i, 1)),
                pl.BlockSpec((length, width), lambda i, s, t: (i, 2)),
                pl.BlockSpec((1, heads, length, 128), lambda i, s, t: (i, 0, 0, 0)),
                pl.BlockSpec((1, heads, 128), lambda i, s, t: (i, 0, 0)),
                matrices,
                matrices,
                pl.BlockSpec((1,) + tails.shape[1:], lambda i, s, t: (i, 0, 0)),
            ],
            out_specs=pl.BlockSpec((1, out_rows, 128), lambda i, s, t: (s[i], 0, 0)),
        ),
        out_shape=pltpu.HBM((requests, out_rows, 128), BF16),
        compiler_params=pltpu.CompilerParams(vmem_limit_bytes=16 << 20),
        cost_estimate=cost(3 << 30, 1 << 16),
        name="stats",
    )(
        places,
        slots,
        *in_hbm([act, act, tail_weight, decay, keys_start, values_start, tails]),
    )


def unpack_kernel(heads, part_ref, *refs):
    keys_ref, values_ref, tail_ref, keys_buf, values_buf, tail_buf, sems = refs[-7:]
    size = 128
    half = heads // 2
    window, columns = tail_ref.shape[1:]
    row = lax.broadcasted_iota(jnp.int32, (size, size), 0)
    col = lax.broadcasted_iota(jnp.int32, (size, size), 1)
    n_parts = part_ref.shape[0]
    under_way = []
    for s in range(n_parts):
        buf = s % 2
        if s >= 2:
            for copy in under_way[s - 2]:
                copy.wait()
        at = (half + heads) * size
        diagonals = part_ref[s, at : at + 16].astype(F32)
        slot = jnp.max(diagonals[half : half + 1]).astype(jnp.int32)
        for p in range(half):
            packed = part_ref[s, p * size : (p + 1) * size].astype(F32)
            turned = packed.T
            keys_buf[buf, p] = jnp.where(row >= col, packed, turned)
            keys_buf[buf, p + half] = jnp.where(
                row < col, packed, jnp.where(row == col, diagonals[p : p + 1], turned)
            )
        for h in range(heads):
            begin = (half + h) * size
            values_buf[buf, h] = part_ref[s, begin : begin + size].astype(F32)
        rows = part_ref[s, at + 16 :].astype(F32)
        strips = [rows[c * window : (c + 1) * window] for c in range(columns // size)]
        tail_buf[s] = jnp.concatenate(strips, axis=1).astype(BF16)
        copies = [
            pltpu.make_async_copy(keys_buf.at[buf], keys_ref.at[slot], sems.at[s, 0]),
            pltpu.make_async_copy(values_buf.at[buf], values_ref.at[slot], sems.at[s, 1]),
            pltpu.make_async_copy(tail_buf.at[s], tail_ref.at[slot], sems.at[s, 2]),
        ]
        for copy in copies:
            copy.start()
        under_way.append(copies)
    for copies in under_way[-2:]:
        for copy in copies:
            copy.wait()


def unpack_call(parts, heads, tail_shape, behind):
    n_parts = parts.shape[0]
    vmem = pl.BlockSpec(memory_space=pltpu.VMEM)
    hbm = pl.BlockSpec(memory_space=pltpu.HBM)
    matrices = jax.ShapeDtypeStruct((n_parts, heads, 128, 128), F32)
    return pl.pallas_call(
        functools.partial(unpack_kernel, heads),
        in_specs=[vmem] + [pl.BlockSpec(memory_space=pl.ANY)] * len(behind),
        out_specs=[hbm, hbm, hbm],
        out_shape=[matrices, matrices, jax.ShapeDtypeStruct((n_parts,) + tail_shape, BF16)],
        scratch_shapes=[
            pltpu.VMEM((2, heads, 128, 128), F32),
            pltpu.VMEM((2, heads, 128, 128), F32),
            pltpu.VMEM((n_parts,) + tail_shape, BF16),
            pltpu.SemaphoreType.DMA((n_parts, 3)),
        ],
        compiler_params=pltpu.CompilerParams(vmem_limit_bytes=16 << 20),
        cost_estimate=cost(3 << 30, 1 << 16),
        name="unpack",
    )(parts, *in_hbm(behind))


def two_terms(values):
    high = values.astype(BF16)
    low = (values - high.astype(F32)).astype(BF16)
    return high, low


def lane_sum(values):
    return jnp.sum(values, axis=-1, keepdims=True)


def cg_kernel(heads, group, ridge_ref, q_ref, k_ref, v_ref, w_ref, c_ref, s_ref, vs_ref, *refs):
    out_ref = refs[-1]
    size = 128
    part = lambda ref, h: ref[:, h * size : (h + 1) * size]
    first_half = lax.broadcasted_iota(jnp.int32, (q_ref.shape[0], size), 1) < size // 2
    transposed = (((1,), (1,)), ((), ()))
    for base in range(0, heads, group):
        hs = range(base, base + group)
        keys = [part(k_ref, h) for h in hs]
        keys2 = [jnp.concatenate([k, k], axis=0) for k in keys]
        keys2_bf = [k.astype(BF16) for k in keys2]
        keys_t = [k.T.astype(BF16) for k in keys2]
        system = []
        for i, h in enumerate(hs):
            m = jnp.concatenate([s_ref[0, h].astype(BF16), keys_t[i]], axis=1)
            system.append(jnp.concatenate([m, m], axis=0))

        def both_terms(field):
            return jnp.concatenate(two_terms(field), axis=1)

        def scored(products, i, h):
            scores = products[:, size:] * w_ref[0, h]
            high = scores.astype(BF16).astype(F32)
            return jnp.where(first_half, high, scores - high).astype(BF16)

        direction = [part(q_ref, h) for h in hs]
        residual = list(direction)
        total = [None] * group
        norm = [lane_sum(r * r) for r in residual]
        for it in range(ITERS):
            products = [
                jnp.dot(both_terms(direction[i]), system[i], preferred_element_type=F32)
                for i in range(group)
            ]
            spread = [
                jnp.dot(scored(products[i], i, h), keys2_bf[i], preferred_element_type=F32)
                for i, h in enumerate(hs)
            ]
            for i, h in enumerate(hs):
                applied = (
                    c_ref[0, h] * products[i][:, :size] + spread[i] + ridge_ref[h] * direction[i]
                )
                step = norm[i] / (lane_sum(direction[i] * applied) + 1e-20)
                moved = step * direction[i]
                total[i] = moved if total[i] is None else total[i] + moved
                if it + 1 < ITERS:
                    residual[i] = residual[i] - step * applied
                    following = lane_sum(residual[i] * residual[i])
                    direction[i] = residual[i] + following / (norm[i] + 1e-20) * direction[i]
                    norm[i] = following
        for i, h in enumerate(hs):
            start_m = jnp.concatenate([vs_ref[0, h].astype(BF16), keys2_bf[i]], axis=0)
            start_m = jnp.concatenate([start_m, start_m], axis=1)
            products = lax.dot_general(
                both_terms(total[i]), start_m, transposed, preferred_element_type=F32
            )
            values = part(v_ref, h)
            values2 = jnp.concatenate([values, values], axis=0).astype(BF16)
            read = c_ref[0, h] * products[:, :size] + jnp.dot(
                scored(products, i, h), values2, preferred_element_type=F32
            )
            out_ref[:, h * size : (h + 1) * size] = read.astype(BF16)


def cg_call(ridge, act, weight2, carried, keys_start, values_start, first, count, held, behind):
    requests, heads = keys_start.shape[:2]
    length, width = act.shape[0] // requests, heads * 128
    per_head = lambda rows: pl.BlockSpec((1, heads, rows, 128), lambda i: (i + first, 0, 0, 0))
    rows_of = lambda which: pl.BlockSpec((length, width), lambda i: (i + first, which))
    inputs = [act, act, act, weight2, carried, keys_start, values_start] + held + behind
    return pl.pallas_call(
        functools.partial(cg_kernel, heads, 8),
        grid=(count,),
        in_specs=[pl.BlockSpec(memory_space=pltpu.SMEM)]
        + [rows_of(0), rows_of(1), rows_of(2)]
        + [per_head(length), per_head(length), per_head(128), per_head(128)]
        + [pl.BlockSpec(memory_space=pl.ANY)] * len(held + behind),
        out_specs=rows_of(0),
        out_shape=jax.ShapeDtypeStruct((requests * length, width), BF16),
        input_output_aliases={8: 0} if held else {},
        compiler_params=pltpu.CompilerParams(vmem_limit_bytes=20 << 20),
        cost_estimate=cost(4 << 30, 1 << 16),
        name="cg",
    )(ridge, *in_hbm(inputs))


def release_kernel(*refs):
    del refs


def release_call(values, behind):
    hbm = pl.BlockSpec(memory_space=pltpu.HBM)
    return pl.pallas_call(
        release_kernel,
        in_specs=[hbm] * len(values) + [pl.BlockSpec(memory_space=pl.ANY)] * len(behind),
        out_specs=[hbm] * len(values),
        out_shape=[pltpu.HBM(value.shape, value.dtype) for value in values],
        input_output_aliases={i: i for i in range(len(values))},
        cost_estimate=cost(1 << 26, 1 << 10),
        name="release",
    )(*in_hbm(values + behind))


def out_kernel(x_ref, tok_ref, gain_ref, w_ref, *refs):
    after_ref, in_ref = refs[-2:]
    attended = jnp.dot(x_ref[...], w_ref[...], preferred_element_type=F32)
    after_attn = (tok_ref[...].astype(F32) + attended).astype(BF16)
    after_ref[...] = after_attn
    in_ref[...] = rms_norm(after_attn.astype(F32), gain_ref[...]).astype(BF16)


def out_call(head_rows, tokens, first, gain, weights, behind):
    rows, width = head_rows.shape[0] // 2, tokens.shape[1]
    half = lambda a: pl.BlockSpec((rows, a.shape[1]), lambda i: (first, 0))
    whole = lambda a: pl.BlockSpec(a.shape, lambda i: (0, 0))
    return pl.pallas_call(
        out_kernel,
        grid=(1,),
        in_specs=[
            half(head_rows),
            half(tokens),
            whole(gain),
            whole(weights),
        ]
        + [pl.BlockSpec(memory_space=pl.ANY)] * len(behind),
        out_specs=[pl.BlockSpec((rows, width), lambda i: (0, 0))] * 2,
        out_shape=[jax.ShapeDtypeStruct((rows, width), BF16)] * 2,
        compiler_params=pltpu.CompilerParams(vmem_limit_bytes=16 << 20),
        cost_estimate=cost(2 << 30, 1 << 16),
        name="out_proj",
    )(*in_hbm([head_rows, tokens, gain, weights] + behind))


def ffn_rows(x, matrices, ready):
    gate_w, up_w, down_w = matrices
    turned = (((1,), (1,)), ((), ()))
    total = None
    for block in range(gate_w.shape[0]):
        ready(block, 0)
        gate = lax.dot_general(x, gate_w[block], turned, preferred_element_type=F32)
        ready(block, 1)
        up = lax.dot_general(x, up_w[block], turned, preferred_element_type=F32)
        hidden = (gate * jax.nn.sigmoid(gate) * up).astype(BF16)
        ready(block, 2)
        sums = jnp.dot(hidden, down_w[block], preferred_element_type=F32)
        total = sums if total is None else total + sums
    return total


def ffn_first_kernel(spans, counts, order_ref, *refs):
    n_in, n_pieces, n_out = counts
    inputs, pieces = refs[:n_in], refs[n_in : n_in + n_pieces]
    outputs, matrices, sems = refs[-4 - n_out : -4], refs[-4:-1], refs[-1]
    size = 128

    def copies(block, which):
        for i, (piece, j) in enumerate(spans[block]):
            to = pl.ds(pl.multiple_of(order_ref[j] * size, size), size)
            yield pltpu.make_async_copy(
                pieces[piece].at[:, pl.ds(which * size, size)],
                matrices[which].at[block, :, to],
                sems.at[block, which, i],
            )

    for block in range(len(spans)):
        for which in range(3):
            for copy in copies(block, which):
                copy.start()

    def ready(block, which):
        for copy in copies(block, which):
            copy.wait()

    x = jnp.concatenate([ref[...] for ref in inputs], axis=0)
    total = ffn_rows(x, matrices, ready)
    begin = 0
    for out_ref in outputs:
        rows = out_ref.shape[0]
        out_ref[...] = total[begin : begin + rows].astype(out_ref.dtype)
        begin += rows


def ffn_first_call(order, spans, inputs, pieces, outputs):
    width = inputs[0].shape[1]
    hidden = pieces[0].shape[0]
    vmem = pl.BlockSpec(memory_space=pltpu.VMEM)
    matrix = pltpu.VMEM((len(spans), hidden, width), BF16)
    counts = (len(inputs), len(pieces), len(outputs))
    return pl.pallas_call(
        functools.partial(ffn_first_kernel, spans, counts),
        grid_spec=pltpu.PrefetchScalarGridSpec(
            num_scalar_prefetch=1,
            grid=(),
            in_specs=[vmem] * len(inputs)
            + [pl.BlockSpec(memory_space=pltpu.HBM)] * len(pieces),
            out_specs=[vmem] * (len(outputs) + 3),
            scratch_shapes=[pltpu.SemaphoreType.DMA((len(spans), 3, len(spans[0])))],
        ),
        out_shape=[jax.ShapeDtypeStruct((rows, width), kind) for rows, kind in outputs]
        + [matrix] * 3,
        compiler_params=pltpu.CompilerParams(vmem_limit_bytes=20 << 20),
        cost_estimate=cost(5 << 30, 1 << 16),
        name="ffn_first",
    )(order, *inputs, *in_hbm(pieces))


def ffn_second_kernel(counts, *refs):
    n_in, n_out = counts
    matrices, outputs = refs[n_in : n_in + 3], refs[-n_out:]
    x = jnp.concatenate([ref[...] for ref in refs[:n_in]], axis=0)
    total = ffn_rows(x, matrices, lambda block, which: None)
    begin = 0
    for out_ref in outputs:
        rows = out_ref.shape[0]
        out_ref[...] = total[begin : begin + rows].astype(out_ref.dtype)
        begin += rows


def ffn_second_call(inputs, matrices, kind, behind):
    vmem = pl.BlockSpec(memory_space=pltpu.VMEM)
    return pl.pallas_call(
        functools.partial(ffn_second_kernel, (len(inputs), len(inputs))),
        in_specs=[vmem] * (len(inputs) + 3)
        + [pl.BlockSpec(memory_space=pl.ANY)] * len(behind),
        out_specs=[vmem] * len(inputs),
        out_shape=[jax.ShapeDtypeStruct(x.shape, kind) for x in inputs],
        compiler_params=pltpu.CompilerParams(vmem_limit_bytes=16 << 20),
        cost_estimate=cost(3 << 30, 1 << 16),
        name="ffn_second",
    )(*inputs, *in_vmem(matrices), *in_hbm(behind))


def sum_kernel(*refs):
    out_ref = refs[-1]
    begin = 0
    for i in range(0, len(refs) - 1, 3):
        after_ref, mine_ref, got_ref = refs[i : i + 3]
        rows = after_ref.shape[0]
        total = after_ref[...].astype(F32) + (mine_ref[...] + got_ref[...].astype(F32))
        out_ref[begin : begin + rows] = total.astype(BF16)
        begin += rows


def sum_call(values):
    vmem = pl.BlockSpec(memory_space=pltpu.VMEM)
    rows = sum(value.shape[0] for value in values[::3])
    return pl.pallas_call(
        sum_kernel,
        in_specs=[vmem] * len(values),
        out_specs=vmem,
        out_shape=jax.ShapeDtypeStruct((rows, values[0].shape[1]), BF16),
        compiler_params=pltpu.CompilerParams(vmem_limit_bytes=8 << 20),
        cost_estimate=cost(1 << 30, 1 << 16),
        name="last_sum",
    )(*values)


def shards(
    tokens,
    lengths,
    ridge_keys,
    ridge_values,
    conv_tail,
    page_table,
    w_qkv,
    conv_weight,
    w_gates,
    decay_rate,
    ridge,
    w_out,
    attn_gain,
    ffn_gain,
    w_gate,
    w_up,
    w_down,
):
    requests, length, width = tokens.shape
    heads = decay_rate.shape[0]
    row_count = requests * length
    reqs, peers = lax.axis_size("req"), lax.axis_size("mesh")
    my_req, my_mesh = lax.axis_index("req"), lax.axis_index("mesh")
    move = lambda value, pairs: lax.ppermute(value, AXES, pairs)
    hop_one, hop_two = flip_mesh(1, reqs, peers), flip_mesh(2, reqs, peers)
    own_rows = w_qkv.shape[0]

    w_out_all = lax.all_gather(w_out, AXES, axis=0, tiled=True)
    flat_tokens = tokens.reshape(row_count, width)
    prep = functools.partial(
        prep_call,
        lengths,
        decay_rate,
        flat_tokens,
        attn_gain,
        w_gates,
        [w_gate.T, w_up.T, w_down],
    )
    ordered = (reqs, peers) == (8, 4)
    core = (my_req % 2).astype(jnp.int32).reshape(1)
    if ordered:
        shifts = {s: shift_mesh(s, reqs, peers) for s in range(1, peers)}
        flips = [flip_req(bit, reqs, peers) for bit in (1, 2, 4)]
        keep, send = split_call(core, w_qkv)
        chip_rows = jnp.concatenate([keep, move(send, flips[0])], axis=0)
        qkv_pieces, places, results, two, last = gather_rows(
            chip_rows, move, shifts, flips[1:], prep
        )
        ffn_own, *prepared = results
        spans, listed = [], []
        for piece, chips in enumerate(places):
            for i, (o, s) in enumerate(chips):
                for other in (0, 1):
                    spans.append((piece, (2 * i + other) * own_rows, own_rows))
                    listed.append((o ^ other, s))
        listed = np.array(listed, np.int32)
        owner = (my_req ^ listed[:, 0]) * peers + (my_mesh - listed[:, 1]) % peers
        qkv_at = (owner * own_rows).astype(jnp.int32)
        (ffn_own,) = release_call([ffn_own], [two])
        ffn_two = move(ffn_own, hop_two)
        (ffn_own,) = release_call([ffn_own], last)
        x_own, y_own = move(ffn_own, flips[1]), move(ffn_own, flips[2])
        normed, weight2, carried, tail_weight, decay = prepared
        mine, theirs = project_call(
            qkv_at, spans, normed, move(normed, flips[0]), qkv_pieces, [ffn_two]
        )
        got = move(theirs, flips[0])
        (ffn_two,) = release_call([ffn_two], [theirs])
        x_two, y_two = move(ffn_two, flips[1]), move(ffn_two, flips[2])
    else:
        w_qkv_all = lax.all_gather(w_qkv, AXES, axis=0, tiled=True)
        qkv_pieces = list(split_call(core, w_qkv_all))
        spans = [(0, 0, w_qkv_all.shape[0])]
        qkv_at = jnp.zeros((1,), jnp.int32)
        _, normed, weight2, carried, tail_weight, decay, _ = prep(w_out, [])
        mine, _ = project_call(qkv_at, spans, normed, normed, qkv_pieces[:1], [])
        got, _ = project_call(qkv_at, spans, normed, normed, qkv_pieces[1:], [])
        gate_all = lax.all_gather(w_gate, "req", axis=0, tiled=True)
        up_all = lax.all_gather(w_up, "req", axis=0, tiled=True)
        down_all = lax.all_gather(w_down, "req", axis=1, tiled=True)
        stripes = width // 128
        ffn_pieces = []
        for j in range(stripes):
            cut = slice(j * 128, (j + 1) * 128)
            piece = jnp.concatenate([gate_all[cut].T, up_all[cut].T, down_all[:, cut]], axis=1)
            ffn_pieces.append(piece)
        ffn_pieces = ffn_pieces + [move(piece, hop_two) for piece in ffn_pieces]
        ffn_spans = [[(i * stripes + j, j) for j in range(stripes)] for i in (0, 1)]
        ffn_order = jnp.arange(stripes)

    held = conv_call(core, lengths, mine, conv_tail, conv_weight, [])
    act, new_tail = conv_call(1 - core, lengths, got, conv_tail, conv_weight, list(held))

    packed = stats_call(
        page_table // requests,
        page_table % requests,
        act,
        tail_weight,
        decay,
        ridge_keys,
        ridge_values,
        new_tail,
    )
    if ordered:
        xy_own, xy_two = move(x_own, flips[2]), move(y_two, flips[1])
        ffn_pieces = [ffn_own, x_own, y_own, xy_own, ffn_two, x_two, y_two, xy_two]
        ffn_pieces = ffn_pieces + [move(p, flips[0]) for p in ffn_pieces]
        ffn_order = my_req ^ np.array((0, 2, 4, 6, 1, 3, 5, 7), np.int32)
        ffn_spans = [
            [(4 * i + j, j) for j in range(4)] + [(8 + 4 * i + j, 4 + j) for j in range(4)]
            for i in (0, 1)
        ]
        behind_a = [x_own, y_own]
        behind_b = [x_two, y_two, xy_own, *ffn_pieces[8:11], ffn_pieces[12]]
        behind_out = [xy_two, ffn_pieces[11], *ffn_pieces[13:15]]
    else:
        behind_a, behind_b, behind_out = [], [], []
    ffn_order = ffn_order.astype(jnp.int32)

    parts = lax.all_to_all(packed, "mesh", split_axis=0, concat_axis=0, tiled=True)

    per = requests // 2
    part_rows = per * length
    gain = ffn_gain.reshape(1, width)
    system = (ridge, act, weight2, carried, ridge_keys, ridge_values)
    heads_a = cg_call(*system, 0, per, [], [packed] + behind_a)
    after_a, in_a = out_call(heads_a, flat_tokens, 0, gain, w_out_all, [])
    theirs_a = move(in_a, hop_one)
    heads_b = cg_call(*system, per, per, [heads_a], [in_a] + behind_b)
    after_b, in_b = out_call(heads_b, flat_tokens, 1, gain, w_out_all, behind_out)
    theirs_b = move(in_b, hop_one)
    for_a, *matrices = ffn_first_call(
        ffn_order, ffn_spans, [theirs_a], ffn_pieces, [(part_rows, BF16)]
    )
    got_a = move(for_a, hop_one)
    (for_b,) = ffn_second_call([theirs_b], matrices, BF16, [for_a])
    got_b = move(for_b, hop_one)
    mine_a, mine_b = ffn_second_call([in_a, in_b], matrices, F32, [for_b])
    keys_decode, values_decode, tail_decode = unpack_call(
        parts, heads, conv_tail.shape[1:], [mine_b]
    )
    mixed = sum_call([after_a, mine_a, got_a, after_b, mine_b, got_b])
    return (
        mixed.reshape(requests, length, width),
        keys_decode,
        values_decode,
        tail_decode,
        heads_b.reshape(requests, length, -1),
    )


def solution(mesh):
    rows = P(AXES)
    in_specs = (
        rows,
        rows,
        rows,
        rows,
        rows,
        rows,
        rows,
        P(),
        P(),
        P(),
        P(),
        rows,
        P(),
        P(),
        P("req", "mesh"),
        P("req", "mesh"),
        P("mesh", "req"),
    )
    out_specs = (rows, rows, rows, rows, rows)
    return jax.shard_map(shards, mesh=mesh, in_specs=in_specs, out_specs=out_specs, check_vma=False)
```

```python
import functools

import jax
import jax.numpy as jnp
import numpy as np
from jax import lax
from jax.experimental import pallas as pl
from jax.experimental.pallas import tpu as pltpu
from jax.sharding import PartitionSpec as P

ITERS = 5
AXES = ("req", "mesh")
TAIL_ROW = 5
F32 = jnp.float32
BF16 = jnp.bfloat16


def rms_norm(values, gain):
    return values * lax.rsqrt(jnp.mean(values * values, axis=-1, keepdims=True) + 1e-05) * gain


def cost(flops, bytes_accessed):
    return pl.CostEstimate(flops=flops, bytes_accessed=bytes_accessed, transcendentals=0)


def in_hbm(values):
    return [pltpu.with_memory_space_constraint(value, pltpu.HBM) for value in values]


def in_vmem(values):
    return [pltpu.with_memory_space_constraint(value, pltpu.VMEM) for value in values]


def flip_req(bit, reqs, peers):
    return [(r * peers + z, (r ^ bit) * peers + z) for r in range(reqs) for z in range(peers)]


def shift_mesh(step, reqs, peers):
    return [(r * peers + z, r * peers + (z + step) % peers) for r in range(reqs) for z in range(peers)]


def flip_mesh(bit, reqs, peers):
    return [(r * peers + z, r * peers + (z ^ bit)) for r in range(reqs) for z in range(peers)]


def gather_rows(own, move, shifts, flips, beside):
    flip_x, flip_y = flips
    rows = own.shape[0]
    one = move(own, shifts[1])
    x_own, y_own = move(own, flip_x), move(own, flip_y)
    three = move(own, shifts[3])
    two = move(one, shifts[1])
    x_one, y_one = move(one, flip_x), move(one, flip_y)
    *results, three = beside(three, [x_own, y_own])
    (two,) = release_call([two], [x_one, y_one])
    rest = jnp.concatenate([three, two], axis=0)
    x_rest, y_rest = move(rest, flip_x), move(rest, flip_y)
    xy_own, xy_one = move(x_own, flip_y), move(y_one, flip_x)
    xy_three, xy_two = move(x_rest[:rows], flip_y), move(y_rest[rows:], flip_x)
    parts = []
    for o, part in ((0, own), (2, x_own), (4, y_own), (6, xy_own)):
        parts.append((part, [(o, 0)]))
    for o, part in ((0, one), (2, x_one), (4, y_one), (6, xy_one)):
        parts.append((part, [(o, 1)]))
    for o, part in ((0, rest), (2, x_rest), (4, y_rest)):
        parts.append((part, [(o, 3), (o, 2)]))
    parts.append((xy_three, [(6, 3)]))
    parts.append((xy_two, [(6, 2)]))
    return [part for part, _ in parts], [where for _, where in parts], results, two, [xy_three, xy_two]


def prep_kernel(heads, len_ref, rate_ref, tok_ref, gain_ref, wg_ref, *refs):
    gate_ref, up_ref, down_ref = refs[:3]
    ffn_ref, normed_ref, weight_ref, carried_ref, tw_ref, decay_ref = refs[-7:-1]
    stripe = down_ref.shape[1]
    if stripe % 128 == 0:
        ffn_ref[:, 0:stripe] = gate_ref[...]
        ffn_ref[:, stripe : 2 * stripe] = up_ref[...]
        ffn_ref[:, 2 * stripe :] = down_ref[...]
    else:
        ffn_ref[...] = jnp.zeros(ffn_ref.shape, BF16)
    requests = weight_ref.shape[0]
    rows = tok_ref.shape[0]
    length = rows // requests
    normed = rms_norm(tok_ref[...].astype(F32), gain_ref[...]).astype(BF16)
    normed_ref[...] = normed
    lane = lax.broadcasted_iota(jnp.int32, (256, 2 * heads), 0)
    column = lax.broadcasted_iota(jnp.int32, (256, 2 * heads), 1)
    chosen = (column == 2 * lane) | ((column == 2 * (lane - 128) + 1) & (lane >= 128))
    gates = jnp.dot(chosen.astype(F32).astype(BF16), wg_ref[...], preferred_element_type=F32)
    logits = lax.dot_general(
        normed, gates.astype(BF16), (((1,), (1,)), ((), ())), preferred_element_type=F32
    )
    rate_lane = lax.broadcasted_iota(jnp.int32, (1, 128), 1)
    rate = jnp.zeros((1, 128), F32)
    for h in range(heads):
        rate = jnp.where(rate_lane == h, rate_ref[h], rate)
    position = lax.broadcasted_iota(jnp.int32, (length, 128), 0)
    lane = lax.broadcasted_iota(jnp.int32, (length, 128), 1)
    slot = jnp.where(lane < length, lane, lane - length)
    causal = position >= slot
    below = lax.broadcasted_iota(jnp.int32, (length, length), 0) >= lax.broadcasted_iota(
        jnp.int32, (length, length), 1
    )
    below = below.astype(F32)
    for r in range(requests):
        mine = logits[r * length : (r + 1) * length]
        live = (position < len_ref[r]).astype(F32)
        beta = jax.nn.sigmoid(mine[:, :128]) * live
        forget = mine[:, 128:]
        softplus = jnp.maximum(forget, 0.0) + jnp.log1p(jnp.exp(-jnp.abs(forget)))
        log_decay = -rate * softplus * live
        cum = jnp.dot(
            below, log_decay, precision=lax.Precision.HIGHEST, preferred_element_type=F32
        )
        last = cum[length - 1 : length]
        cum_rows = jnp.concatenate([cum, cum], axis=0).T
        beta_rows = jnp.concatenate([beta, beta], axis=0).T
        carried = jnp.exp(cum)
        tail_weight = jnp.exp(last - cum) * beta
        decay = jnp.exp(last)
        for h in range(heads):
            spread = cum[:, h : h + 1] - cum_rows[h : h + 1]
            weight = jnp.where(causal, jnp.exp(jnp.minimum(spread, 0.0)), 0.0)
            weight_ref[r, h] = weight * beta_rows[h : h + 1]
            carried_ref[r, h] = jnp.broadcast_to(carried[:, h : h + 1], (length, 128))
            tw_ref[r, h] = jnp.broadcast_to(tail_weight[:, h : h + 1], (length, 128))
            decay_ref[r, h : h + 1] = jnp.broadcast_to(decay[:, h : h + 1], (1, 128))


def prep_call(lengths, decay_rate, tokens, gain, w_gates, ffn_weights, through, behind):
    rows, width = tokens.shape
    requests, heads = lengths.shape[0], decay_rate.shape[0]
    length = rows // requests
    smem = pl.BlockSpec(memory_space=pltpu.SMEM)
    hbm = pl.BlockSpec(memory_space=pltpu.HBM)
    whole = lambda shape: pl.BlockSpec(shape, lambda i: (0,) * len(shape))
    inputs = [tokens, gain.reshape(1, width), w_gates.T, *ffn_weights]
    hidden, stripe = ffn_weights[0].shape
    wide = (requests, heads, length, 128)
    shapes = [(hidden, 3 * stripe), (rows, width), wide, wide, wide, (requests, heads, 128)]
    return pl.pallas_call(
        functools.partial(prep_kernel, heads),
        grid=(1,),
        in_specs=[smem] * 2 + [whole(value.shape) for value in inputs] + [hbm] * (1 + len(behind)),
        out_specs=[whole(shape) for shape in shapes] + [hbm],
        out_shape=[pltpu.HBM(shape, F32 if i > 1 else BF16) for i, shape in enumerate(shapes)]
        + [pltpu.HBM(through.shape, through.dtype)],
        input_output_aliases={2 + len(inputs): len(shapes)},
        compiler_params=pltpu.CompilerParams(vmem_limit_bytes=20 << 20),
        cost_estimate=cost(3 << 30, 1 << 16),
        name="norm_gates",
    )(lengths, decay_rate, *in_hbm(inputs + [through] + behind))


def split_kernel(core_ref, w_ref, keep_ref, send_ref):
    wide = keep_ref.shape[1] // 3
    for which in range(3):
        to = slice(which * wide, (which + 1) * wide)
        for out_ref, half in ((keep_ref, core_ref[0]), (send_ref, 1 - core_ref[0])):
            begin = pl.multiple_of((2 * which + half) * wide, wide)
            out_ref[:, to] = w_ref[:, pl.ds(begin, wide)]


def split_call(core, weights):
    rows, columns = weights.shape
    vmem = pl.BlockSpec(memory_space=pltpu.VMEM)
    return pl.pallas_call(
        split_kernel,
        in_specs=[pl.BlockSpec(memory_space=pltpu.SMEM), vmem],
        out_specs=[vmem] * 2,
        out_shape=[jax.ShapeDtypeStruct((rows, columns // 2), BF16)] * 2,
        cost_estimate=cost(1 << 28, 1 << 16),
        name="split_heads",
    )(core, weights)


def project_kernel(n_pieces, spans, at_ref, x_ref, other_ref, *refs):
    pieces = refs[:n_pieces]
    mine_ref, theirs_ref, weights, sems = refs[-4:]
    step = pl.program_id(0)
    columns = mine_ref.shape[1]
    chunks = weights.shape[1] // columns

    def copies(c):
        cut = pl.ds(c * columns, columns)
        for i, (piece, first, rows) in enumerate(spans):
            begin = pl.multiple_of(at_ref[i], 16)
            yield pltpu.make_async_copy(
                pieces[piece].at[pl.ds(first, rows), cut],
                weights.at[pl.ds(begin, rows), cut],
                sems.at[c, i],
            )

    @pl.when(step == 0)
    def _():
        for c in range(chunks):
            for copy in copies(c):
                copy.start()

    for c in range(chunks):

        @pl.when(step == c)
        def _():
            for copy in copies(c):
                copy.wait()

    now = weights[:, pl.ds(pl.multiple_of(step * columns, columns), columns)]
    theirs = jnp.dot(other_ref[...], now, preferred_element_type=F32)
    theirs_ref[...] = theirs.astype(BF16)
    mine_ref[...] = jnp.dot(x_ref[...], now, preferred_element_type=F32).astype(BF16)


def project_call(at, spans, x, other, pieces, behind):
    rows, depth = x.shape
    columns = pieces[0].shape[1]
    wide = 512
    whole = pl.BlockSpec(x.shape, lambda j, s: (0, 0))
    block = pl.BlockSpec((rows, wide), lambda j, s: (0, j))
    return pl.pallas_call(
        functools.partial(project_kernel, len(pieces), spans),
        grid_spec=pltpu.PrefetchScalarGridSpec(
            num_scalar_prefetch=1,
            grid=(columns // wide,),
            in_specs=[whole, whole] + [pl.BlockSpec(memory_space=pltpu.HBM)] * len(pieces + behind),
            out_specs=[block, block],
            scratch_shapes=[
                pltpu.VMEM((depth, columns), BF16),
                pltpu.SemaphoreType.DMA((columns // wide, len(spans))),
            ],
        ),
        out_shape=[pltpu.HBM((rows, columns), BF16)] * 2,
        compiler_params=pltpu.CompilerParams(vmem_limit_bytes=16 << 20),
        cost_estimate=cost(3 << 30, 1 << 16),
        name="project",
    )(at, *in_hbm([x, other] + pieces + behind))


def conv_kernel(half_ref, len_ref, projected_ref, tail_ref, conv_ref, *refs):
    act_ref, new_tail_ref = refs[-2:]
    requests, window, columns = tail_ref.shape
    length = projected_ref.shape[0] // requests
    is_vector = pl.program_id(0) < 2
    for r in range(requests):
        blank = jnp.zeros((TAIL_ROW, columns), F32)
        head_rows = jnp.concatenate([blank, tail_ref[r].astype(F32)], axis=0)
        mine = projected_ref[r * length : (r + 1) * length].astype(F32)
        extended = jnp.concatenate([head_rows, mine], axis=0)
        wanted = lax.broadcasted_iota(jnp.int32, (8, extended.shape[0]), 0) + len_ref[r]
        place = lax.broadcasted_iota(jnp.int32, (8, extended.shape[0]), 1)
        chosen = (place == wanted + TAIL_ROW).astype(F32)
        rows = jnp.dot(chosen, extended, preferred_element_type=F32)
        new_tail_ref[r] = rows[:window].astype(BF16)
        total = conv_ref[0:1] * extended[TAIL_ROW : TAIL_ROW + length]
        for tap in range(1, window + 1):
            total = total + conv_ref[tap : tap + 1] * extended[
                TAIL_ROW + tap : TAIL_ROW + tap + length
            ]
        act = total * jax.nn.sigmoid(total)
        for h in range(columns // 128):
            head = act[:, h * 128 : (h + 1) * 128]
            scale = lax.rsqrt(jnp.sum(head * head, axis=-1, keepdims=True) + 1e-06)
            scale = jnp.where(is_vector, scale, jnp.ones_like(scale))
            act_ref[r * length : (r + 1) * length, h * 128 : (h + 1) * 128] = head * scale


def conv_call(half, lengths, projected, tails, conv_weight, held):
    rows, columns = projected.shape
    requests, window = tails.shape[:2]
    wide = columns // 3
    rows_block = pl.BlockSpec((rows, wide), lambda j, s, t: (0, 2 * j + s[0]))
    tail_block = pl.BlockSpec((requests, window, wide), lambda j, s, t: (0, 0, 2 * j + s[0]))
    return pl.pallas_call(
        conv_kernel,
        grid_spec=pltpu.PrefetchScalarGridSpec(
            num_scalar_prefetch=2,
            grid=(3,),
            in_specs=[
                pl.BlockSpec((rows, wide), lambda j, s, t: (0, j)),
                tail_block,
                pl.BlockSpec((window + 1, wide), lambda j, s, t: (0, 2 * j + s[0])),
            ]
            + [pl.BlockSpec(memory_space=pl.ANY)] * len(held),
            out_specs=[rows_block, tail_block],
        ),
        out_shape=[
            pltpu.HBM((rows, 2 * columns), F32),
            pltpu.HBM(tails.shape, BF16),
        ],
        input_output_aliases={5: 0, 6: 1} if held else {},
        compiler_params=pltpu.CompilerParams(vmem_limit_bytes=16 << 20),
        cost_estimate=cost(2 << 30, 1 << 16),
        name="conv_norm",
    )(half, lengths, *in_hbm([projected, tails, conv_weight] + held))


def stats_kernel(heads, place_ref, slot_ref, k_ref, v_ref, tw_ref, fd_ref, s_ref, vs_ref, *refs):
    tail_ref, out_ref = refs
    size = 128
    row = lax.broadcasted_iota(jnp.int32, (size, size), 0)
    col = lax.broadcasted_iota(jnp.int32, (size, size), 1)
    half = heads // 2
    contract = (((0,), (0,)), ((), ()))
    keys_end = []
    for h in range(heads):
        keys = k_ref[:, h * size : (h + 1) * size]
        values = v_ref[:, h * size : (h + 1) * size]
        tail_weight = tw_ref[0, h]
        both = jnp.concatenate([keys * tail_weight, values * tail_weight], axis=1).astype(BF16)
        sums = lax.dot_general(both, keys.astype(BF16), contract, preferred_element_type=F32)
        decay = fd_ref[0, h : h + 1]
        keys_end.append(decay * s_ref[0, h] + sums[:size])
        at = half * size + h * size
        out_ref[0, at : at + size] = (decay * vs_ref[0, h] + sums[size:]).astype(BF16)
    diagonals = []
    for p in range(half):
        low, high = keys_end[p], keys_end[p + half]
        out_ref[0, p * size : (p + 1) * size] = jnp.where(row >= col, low, high).astype(BF16)
        diagonals.append(jnp.sum(jnp.where(row == col, high, 0.0), axis=0, keepdims=True))
    at = (half + heads) * size
    slot = slot_ref[pl.program_id(0)].astype(F32)
    diagonals.append(jnp.full((16 - half, size), slot, F32))
    out_ref[0, at : at + 16] = jnp.concatenate(diagonals, axis=0).astype(BF16)
    tail = tail_ref[0].astype(F32)
    strips = [tail[:, c : c + size] for c in range(0, tail.shape[1], size)]
    fill = out_ref.shape[1] - at - 16 - len(strips) * tail.shape[0]
    strips.append(jnp.zeros((fill, size), F32))
    out_ref[0, at + 16 :] = jnp.concatenate(strips, axis=0).astype(BF16)


def stats_call(places, slots, act, tail_weight, decay, keys_start, values_start, tails):
    requests, heads = keys_start.shape[:2]
    length, width = act.shape[0] // requests, heads * 128
    tail_rows = tails.shape[1] * tails.shape[2] // 128
    out_rows = (heads // 2 + heads) * 128 + 16 + tail_rows + -tail_rows % 16
    matrices = pl.BlockSpec((1, heads, 128, 128), lambda i, s, t: (i, 0, 0, 0))
    return pl.pallas_call(
        functools.partial(stats_kernel, heads),
        grid_spec=pltpu.PrefetchScalarGridSpec(
            num_scalar_prefetch=2,
            grid=(requests,),
            in_specs=[
                pl.BlockSpec((length, width), lambda i, s, t: (i, 1)),
                pl.BlockSpec((length, width), lambda i, s, t: (i, 2)),
                pl.BlockSpec((1, heads, length, 128), lambda i, s, t: (i, 0, 0, 0)),
                pl.BlockSpec((1, heads, 128), lambda i, s, t: (i, 0, 0)),
                matrices,
                matrices,
                pl.BlockSpec((1,) + tails.shape[1:], lambda i, s, t: (i, 0, 0)),
            ],
            out_specs=pl.BlockSpec((1, out_rows, 128), lambda i, s, t: (s[i], 0, 0)),
        ),
        out_shape=pltpu.HBM((requests, out_rows, 128), BF16),
        compiler_params=pltpu.CompilerParams(vmem_limit_bytes=16 << 20),
        cost_estimate=cost(3 << 30, 1 << 16),
        name="stats",
    )(
        places,
        slots,
        *in_hbm([act, act, tail_weight, decay, keys_start, values_start, tails]),
    )


def unpack_kernel(heads, part_ref, *refs):
    keys_ref, values_ref, tail_ref, keys_buf, values_buf, tail_buf, sems = refs[-7:]
    size = 128
    half = heads // 2
    window, columns = tail_ref.shape[1:]
    row = lax.broadcasted_iota(jnp.int32, (size, size), 0)
    col = lax.broadcasted_iota(jnp.int32, (size, size), 1)
    n_parts = part_ref.shape[0]
    under_way = []
    for s in range(n_parts):
        buf = s % 2
        if s >= 2:
            for copy in under_way[s - 2]:
                copy.wait()
        at = (half + heads) * size
        diagonals = part_ref[s, at : at + 16].astype(F32)
        slot = jnp.max(diagonals[half : half + 1]).astype(jnp.int32)
        for p in range(half):
            packed = part_ref[s, p * size : (p + 1) * size].astype(F32)
            turned = packed.T
            keys_buf[buf, p] = jnp.where(row >= col, packed, turned)
            keys_buf[buf, p + half] = jnp.where(
                row < col, packed, jnp.where(row == col, diagonals[p : p + 1], turned)
            )
        for h in range(heads):
            begin = (half + h) * size
            values_buf[buf, h] = part_ref[s, begin : begin + size].astype(F32)
        rows = part_ref[s, at + 16 :].astype(F32)
        strips = [rows[c * window : (c + 1) * window] for c in range(columns // size)]
        tail_buf[s] = jnp.concatenate(strips, axis=1).astype(BF16)
        copies = [
            pltpu.make_async_copy(keys_buf.at[buf], keys_ref.at[slot], sems.at[s, 0]),
            pltpu.make_async_copy(values_buf.at[buf], values_ref.at[slot], sems.at[s, 1]),
            pltpu.make_async_copy(tail_buf.at[s], tail_ref.at[slot], sems.at[s, 2]),
        ]
        for copy in copies:
            copy.start()
        under_way.append(copies)
    for copies in under_way[-2:]:
        for copy in copies:
            copy.wait()


def unpack_call(parts, heads, tail_shape, behind):
    n_parts = parts.shape[0]
    vmem = pl.BlockSpec(memory_space=pltpu.VMEM)
    hbm = pl.BlockSpec(memory_space=pltpu.HBM)
    matrices = jax.ShapeDtypeStruct((n_parts, heads, 128, 128), F32)
    return pl.pallas_call(
        functools.partial(unpack_kernel, heads),
        in_specs=[vmem] + [pl.BlockSpec(memory_space=pl.ANY)] * len(behind),
        out_specs=[hbm, hbm, hbm],
        out_shape=[matrices, matrices, jax.ShapeDtypeStruct((n_parts,) + tail_shape, BF16)],
        scratch_shapes=[
            pltpu.VMEM((2, heads, 128, 128), F32),
            pltpu.VMEM((2, heads, 128, 128), F32),
            pltpu.VMEM((n_parts,) + tail_shape, BF16),
            pltpu.SemaphoreType.DMA((n_parts, 3)),
        ],
        compiler_params=pltpu.CompilerParams(vmem_limit_bytes=16 << 20),
        cost_estimate=cost(3 << 30, 1 << 16),
        name="unpack",
    )(parts, *in_hbm(behind))


def two_terms(values):
    high = values.astype(BF16)
    low = (values - high.astype(F32)).astype(BF16)
    return high, low


def lane_sum(values):
    return jnp.sum(values, axis=-1, keepdims=True)


def cg_kernel(heads, group, ridge_ref, q_ref, k_ref, v_ref, w_ref, c_ref, s_ref, vs_ref, *refs):
    out_ref = refs[-1]
    size = 128
    part = lambda ref, h: ref[:, h * size : (h + 1) * size]
    first_half = lax.broadcasted_iota(jnp.int32, (q_ref.shape[0], size), 1) < size // 2
    transposed = (((1,), (1,)), ((), ()))
    for base in range(0, heads, group):
        hs = range(base, base + group)
        keys = [part(k_ref, h) for h in hs]
        keys2 = [jnp.concatenate([k, k], axis=0) for k in keys]
        keys2_bf = [k.astype(BF16) for k in keys2]
        keys_t = [k.T.astype(BF16) for k in keys2]
        system = []
        for i, h in enumerate(hs):
            m = jnp.concatenate([s_ref[0, h].astype(BF16), keys_t[i]], axis=1)
            system.append(m)

        def both_terms(field):
            return jnp.concatenate(two_terms(field), axis=0)

        def joined(products):
            rows = products.shape[0] // 2
            return products[:rows] + products[rows:]

        def scored(products, i, h):
            scores = products[:, size:] * w_ref[0, h]
            high = scores.astype(BF16).astype(F32)
            return jnp.where(first_half, high, scores - high).astype(BF16)

        direction = [part(q_ref, h) for h in hs]
        residual = list(direction)
        total = [None] * group
        norm = [lane_sum(r * r) for r in residual]
        for it in range(ITERS):
            products = [
                joined(jnp.dot(both_terms(direction[i]), system[i], preferred_element_type=F32))
                for i in range(group)
            ]
            spread = [
                jnp.dot(scored(products[i], i, h), keys2_bf[i], preferred_element_type=F32)
                for i, h in enumerate(hs)
            ]
            for i, h in enumerate(hs):
                applied = (
                    c_ref[0, h] * products[i][:, :size] + spread[i] + ridge_ref[h] * direction[i]
                )
                step = norm[i] / (lane_sum(direction[i] * applied) + 1e-20)
                moved = step * direction[i]
                total[i] = moved if total[i] is None else total[i] + moved
                if it + 1 < ITERS:
                    residual[i] = residual[i] - step * applied
                    following = lane_sum(residual[i] * residual[i])
                    direction[i] = residual[i] + following / (norm[i] + 1e-20) * direction[i]
                    norm[i] = following
        for i, h in enumerate(hs):
            start_m = jnp.concatenate([vs_ref[0, h].astype(BF16), keys2_bf[i]], axis=0)
            products = joined(
                lax.dot_general(
                    both_terms(total[i]), start_m, transposed, preferred_element_type=F32
                )
            )
            values = part(v_ref, h)
            values2 = jnp.concatenate([values, values], axis=0).astype(BF16)
            read = c_ref[0, h] * products[:, :size] + jnp.dot(
                scored(products, i, h), values2, preferred_element_type=F32
            )
            out_ref[:, h * size : (h + 1) * size] = read.astype(BF16)


def cg_call(ridge, act, weight2, carried, keys_start, values_start, first, count, held, behind):
    requests, heads = keys_start.shape[:2]
    length, width = act.shape[0] // requests, heads * 128
    per_head = lambda rows: pl.BlockSpec((1, heads, rows, 128), lambda i: (i + first, 0, 0, 0))
    rows_of = lambda which: pl.BlockSpec((length, width), lambda i: (i + first, which))
    inputs = [act, act, act, weight2, carried, keys_start, values_start] + held + behind
    return pl.pallas_call(
        functools.partial(cg_kernel, heads, 8),
        grid=(count,),
        in_specs=[pl.BlockSpec(memory_space=pltpu.SMEM)]
        + [rows_of(0), rows_of(1), rows_of(2)]
        + [per_head(length), per_head(length), per_head(128), per_head(128)]
        + [pl.BlockSpec(memory_space=pl.ANY)] * len(held + behind),
        out_specs=rows_of(0),
        out_shape=jax.ShapeDtypeStruct((requests * length, width), BF16),
        input_output_aliases={8: 0} if held else {},
        compiler_params=pltpu.CompilerParams(vmem_limit_bytes=20 << 20),
        cost_estimate=cost(4 << 30, 1 << 16),
        name="cg",
    )(ridge, *in_hbm(inputs))


def release_kernel(*refs):
    del refs


def release_call(values, behind):
    hbm = pl.BlockSpec(memory_space=pltpu.HBM)
    return pl.pallas_call(
        release_kernel,
        in_specs=[hbm] * len(values) + [pl.BlockSpec(memory_space=pl.ANY)] * len(behind),
        out_specs=[hbm] * len(values),
        out_shape=[pltpu.HBM(value.shape, value.dtype) for value in values],
        input_output_aliases={i: i for i in range(len(values))},
        cost_estimate=cost(1 << 26, 1 << 10),
        name="release",
    )(*in_hbm(values + behind))


def out_kernel(x_ref, tok_ref, gain_ref, w_ref, *refs):
    after_ref, in_ref = refs[-2:]
    attended = jnp.dot(x_ref[...], w_ref[...], preferred_element_type=F32)
    after_attn = (tok_ref[...].astype(F32) + attended).astype(BF16)
    after_ref[...] = after_attn
    in_ref[...] = rms_norm(after_attn.astype(F32), gain_ref[...]).astype(BF16)


def out_call(head_rows, tokens, first, gain, weights, behind):
    rows, width = head_rows.shape[0] // 2, tokens.shape[1]
    half = lambda a: pl.BlockSpec((rows, a.shape[1]), lambda i: (first, 0))
    whole = lambda a: pl.BlockSpec(a.shape, lambda i: (0, 0))
    return pl.pallas_call(
        out_kernel,
        grid=(1,),
        in_specs=[
            half(head_rows),
            half(tokens),
            whole(gain),
            whole(weights),
        ]
        + [pl.BlockSpec(memory_space=pl.ANY)] * len(behind),
        out_specs=[pl.BlockSpec((rows, width), lambda i: (0, 0))] * 2,
        out_shape=[jax.ShapeDtypeStruct((rows, width), BF16)] * 2,
        compiler_params=pltpu.CompilerParams(vmem_limit_bytes=16 << 20),
        cost_estimate=cost(2 << 30, 1 << 16),
        name="out_proj",
    )(*in_hbm([head_rows, tokens, gain, weights] + behind))


def ffn_rows(x, matrices, ready):
    gate_w, up_w, down_w = matrices
    turned = (((1,), (1,)), ((), ()))
    total = None
    for block in range(gate_w.shape[0]):
        ready(block, 0)
        gate = lax.dot_general(x, gate_w[block], turned, preferred_element_type=F32)
        ready(block, 1)
        up = lax.dot_general(x, up_w[block], turned, preferred_element_type=F32)
        hidden = (gate * jax.nn.sigmoid(gate) * up).astype(BF16)
        ready(block, 2)
        sums = jnp.dot(hidden, down_w[block], preferred_element_type=F32)
        total = sums if total is None else total + sums
    return total


def ffn_first_kernel(spans, counts, order_ref, *refs):
    n_in, n_pieces, n_out = counts
    inputs, pieces = refs[:n_in], refs[n_in : n_in + n_pieces]
    outputs, matrices, sems = refs[-4 - n_out : -4], refs[-4:-1], refs[-1]
    size = 128

    def copies(block, which):
        for i, (piece, j) in enumerate(spans[block]):
            to = pl.ds(pl.multiple_of(order_ref[j] * size, size), size)
            yield pltpu.make_async_copy(
                pieces[piece].at[:, pl.ds(which * size, size)],
                matrices[which].at[block, :, to],
                sems.at[block, which, i],
            )

    for block in range(len(spans)):
        for which in range(3):
            for copy in copies(block, which):
                copy.start()

    def ready(block, which):
        for copy in copies(block, which):
            copy.wait()

    x = jnp.concatenate([ref[...] for ref in inputs], axis=0)
    total = ffn_rows(x, matrices, ready)
    begin = 0
    for out_ref in outputs:
        rows = out_ref.shape[0]
        out_ref[...] = total[begin : begin + rows].astype(out_ref.dtype)
        begin += rows


def ffn_first_call(order, spans, inputs, pieces, outputs):
    width = inputs[0].shape[1]
    hidden = pieces[0].shape[0]
    vmem = pl.BlockSpec(memory_space=pltpu.VMEM)
    matrix = pltpu.VMEM((len(spans), hidden, width), BF16)
    counts = (len(inputs), len(pieces), len(outputs))
    return pl.pallas_call(
        functools.partial(ffn_first_kernel, spans, counts),
        grid_spec=pltpu.PrefetchScalarGridSpec(
            num_scalar_prefetch=1,
            grid=(),
            in_specs=[vmem] * len(inputs)
            + [pl.BlockSpec(memory_space=pltpu.HBM)] * len(pieces),
            out_specs=[vmem] * (len(outputs) + 3),
            scratch_shapes=[pltpu.SemaphoreType.DMA((len(spans), 3, len(spans[0])))],
        ),
        out_shape=[jax.ShapeDtypeStruct((rows, width), kind) for rows, kind in outputs]
        + [matrix] * 3,
        compiler_params=pltpu.CompilerParams(vmem_limit_bytes=20 << 20),
        cost_estimate=cost(5 << 30, 1 << 16),
        name="ffn_first",
    )(order, *inputs, *in_hbm(pieces))


def ffn_second_kernel(counts, *refs):
    n_in, n_out = counts
    matrices, outputs = refs[n_in : n_in + 3], refs[-n_out:]
    x = jnp.concatenate([ref[...] for ref in refs[:n_in]], axis=0)
    total = ffn_rows(x, matrices, lambda block, which: None)
    begin = 0
    for out_ref in outputs:
        rows = out_ref.shape[0]
        out_ref[...] = total[begin : begin + rows].astype(out_ref.dtype)
        begin += rows


def ffn_second_call(inputs, matrices, kind, behind):
    vmem = pl.BlockSpec(memory_space=pltpu.VMEM)
    return pl.pallas_call(
        functools.partial(ffn_second_kernel, (len(inputs), len(inputs))),
        in_specs=[vmem] * (len(inputs) + 3)
        + [pl.BlockSpec(memory_space=pl.ANY)] * len(behind),
        out_specs=[vmem] * len(inputs),
        out_shape=[jax.ShapeDtypeStruct(x.shape, kind) for x in inputs],
        compiler_params=pltpu.CompilerParams(vmem_limit_bytes=16 << 20),
        cost_estimate=cost(3 << 30, 1 << 16),
        name="ffn_second",
    )(*inputs, *in_vmem(matrices), *in_hbm(behind))


def sum_kernel(*refs):
    out_ref = refs[-1]
    begin = 0
    for i in range(0, len(refs) - 1, 3):
        after_ref, mine_ref, got_ref = refs[i : i + 3]
        rows = after_ref.shape[0]
        total = after_ref[...].astype(F32) + (mine_ref[...] + got_ref[...].astype(F32))
        out_ref[begin : begin + rows] = total.astype(BF16)
        begin += rows


def sum_call(values):
    vmem = pl.BlockSpec(memory_space=pltpu.VMEM)
    rows = sum(value.shape[0] for value in values[::3])
    return pl.pallas_call(
        sum_kernel,
        in_specs=[vmem] * len(values),
        out_specs=vmem,
        out_shape=jax.ShapeDtypeStruct((rows, values[0].shape[1]), BF16),
        compiler_params=pltpu.CompilerParams(vmem_limit_bytes=8 << 20),
        cost_estimate=cost(1 << 30, 1 << 16),
        name="last_sum",
    )(*values)


def shards(
    tokens,
    lengths,
    ridge_keys,
    ridge_values,
    conv_tail,
    page_table,
    w_qkv,
    conv_weight,
    w_gates,
    decay_rate,
    ridge,
    w_out,
    attn_gain,
    ffn_gain,
    w_gate,
    w_up,
    w_down,
):
    requests, length, width = tokens.shape
    heads = decay_rate.shape[0]
    row_count = requests * length
    reqs, peers = lax.axis_size("req"), lax.axis_size("mesh")
    my_req, my_mesh = lax.axis_index("req"), lax.axis_index("mesh")
    move = lambda value, pairs: lax.ppermute(value, AXES, pairs)
    hop_one, hop_two = flip_mesh(1, reqs, peers), flip_mesh(2, reqs, peers)
    own_rows = w_qkv.shape[0]

    w_out_all = lax.all_gather(w_out, AXES, axis=0, tiled=True)
    flat_tokens = tokens.reshape(row_count, width)
    prep = functools.partial(
        prep_call,
        lengths,
        decay_rate,
        flat_tokens,
        attn_gain,
        w_gates,
        [w_gate.T, w_up.T, w_down],
    )
    ordered = (reqs, peers) == (8, 4)
    core = (my_req % 2).astype(jnp.int32).reshape(1)
    if ordered:
        shifts = {s: shift_mesh(s, reqs, peers) for s in range(1, peers)}
        flips = [flip_req(bit, reqs, peers) for bit in (1, 2, 4)]
        keep, send = split_call(core, w_qkv)
        chip_rows = jnp.concatenate([keep, move(send, flips[0])], axis=0)
        qkv_pieces, places, results, two, last = gather_rows(
            chip_rows, move, shifts, flips[1:], prep
        )
        ffn_own, *prepared = results
        spans, listed = [], []
        for piece, chips in enumerate(places):
            for i, (o, s) in enumerate(chips):
                for other in (0, 1):
                    spans.append((piece, (2 * i + other) * own_rows, own_rows))
                    listed.append((o ^ other, s))
        listed = np.array(listed, np.int32)
        owner = (my_req ^ listed[:, 0]) * peers + (my_mesh - listed[:, 1]) % peers
        qkv_at = (owner * own_rows).astype(jnp.int32)
        (ffn_own,) = release_call([ffn_own], [two])
        ffn_two = move(ffn_own, hop_two)
        (ffn_own,) = release_call([ffn_own], last)
        x_own, y_own = move(ffn_own, flips[1]), move(ffn_own, flips[2])
        normed, weight2, carried, tail_weight, decay = prepared
        mine, theirs = project_call(
            qkv_at, spans, normed, move(normed, flips[0]), qkv_pieces, [ffn_two]
        )
        got = move(theirs, flips[0])
        (ffn_two,) = release_call([ffn_two], [theirs])
        x_two, y_two = move(ffn_two, flips[1]), move(ffn_two, flips[2])
    else:
        w_qkv_all = lax.all_gather(w_qkv, AXES, axis=0, tiled=True)
        qkv_pieces = list(split_call(core, w_qkv_all))
        spans = [(0, 0, w_qkv_all.shape[0])]
        qkv_at = jnp.zeros((1,), jnp.int32)
        _, normed, weight2, carried, tail_weight, decay, _ = prep(w_out, [])
        mine, _ = project_call(qkv_at, spans, normed, normed, qkv_pieces[:1], [])
        got, _ = project_call(qkv_at, spans, normed, normed, qkv_pieces[1:], [])
        gate_all = lax.all_gather(w_gate, "req", axis=0, tiled=True)
        up_all = lax.all_gather(w_up, "req", axis=0, tiled=True)
        down_all = lax.all_gather(w_down, "req", axis=1, tiled=True)
        stripes = width // 128
        ffn_pieces = []
        for j in range(stripes):
            cut = slice(j * 128, (j + 1) * 128)
            piece = jnp.concatenate([gate_all[cut].T, up_all[cut].T, down_all[:, cut]], axis=1)
            ffn_pieces.append(piece)
        ffn_pieces = ffn_pieces + [move(piece, hop_two) for piece in ffn_pieces]
        ffn_spans = [[(i * stripes + j, j) for j in range(stripes)] for i in (0, 1)]
        ffn_order = jnp.arange(stripes)

    held = conv_call(core, lengths, mine, conv_tail, conv_weight, [])
    act, new_tail = conv_call(1 - core, lengths, got, conv_tail, conv_weight, list(held))

    packed = stats_call(
        page_table // requests,
        page_table % requests,
        act,
        tail_weight,
        decay,
        ridge_keys,
        ridge_values,
        new_tail,
    )
    if ordered:
        xy_own, xy_two = move(x_own, flips[2]), move(y_two, flips[1])
        ffn_pieces = [ffn_own, x_own, y_own, xy_own, ffn_two, x_two, y_two, xy_two]
        ffn_pieces = ffn_pieces + [move(p, flips[0]) for p in ffn_pieces]
        ffn_order = my_req ^ np.array((0, 2, 4, 6, 1, 3, 5, 7), np.int32)
        ffn_spans = [
            [(4 * i + j, j) for j in range(4)] + [(8 + 4 * i + j, 4 + j) for j in range(4)]
            for i in (0, 1)
        ]
        behind_a = [x_own, y_own]
        behind_b = [x_two, y_two, xy_own, *ffn_pieces[8:11], ffn_pieces[12]]
        behind_out = [xy_two, ffn_pieces[11], *ffn_pieces[13:15]]
    else:
        behind_a, behind_b, behind_out = [], [], []
    ffn_order = ffn_order.astype(jnp.int32)

    parts = lax.all_to_all(packed, "mesh", split_axis=0, concat_axis=0, tiled=True)

    per = requests // 2
    part_rows = per * length
    gain = ffn_gain.reshape(1, width)
    system = (ridge, act, weight2, carried, ridge_keys, ridge_values)
    heads_a = cg_call(*system, 0, per, [], [packed] + behind_a)
    after_a, in_a = out_call(heads_a, flat_tokens, 0, gain, w_out_all, [])
    theirs_a = move(in_a, hop_one)
    heads_b = cg_call(*system, per, per, [heads_a], [in_a] + behind_b)
    after_b, in_b = out_call(heads_b, flat_tokens, 1, gain, w_out_all, behind_out)
    theirs_b = move(in_b, hop_one)
    for_a, *matrices = ffn_first_call(
        ffn_order, ffn_spans, [theirs_a], ffn_pieces, [(part_rows, BF16)]
    )
    got_a = move(for_a, hop_one)
    (for_b,) = ffn_second_call([theirs_b], matrices, BF16, [for_a])
    got_b = move(for_b, hop_one)
    mine_a, mine_b = ffn_second_call([in_a, in_b], matrices, F32, [for_b])
    keys_decode, values_decode, tail_decode = unpack_call(
        parts, heads, conv_tail.shape[1:], [mine_b]
    )
    mixed = sum_call([after_a, mine_a, got_a, after_b, mine_b, got_b])
    return (
        mixed.reshape(requests, length, width),
        keys_decode,
        values_decode,
        tail_decode,
        heads_b.reshape(requests, length, -1),
    )


def solution(mesh):
    rows = P(AXES)
    in_specs = (
        rows,
        rows,
        rows,
        rows,
        rows,
        rows,
        rows,
        P(),
        P(),
        P(),
        P(),
        rows,
        P(),
        P(),
        P("req", "mesh"),
        P("req", "mesh"),
        P("mesh", "req"),
    )
    out_specs = (rows, rows, rows, rows, rows)
    return jax.shard_map(shards, mesh=mesh, in_specs=in_specs, out_specs=out_specs, check_vma=False)
```

```python
import functools

import jax
import jax.numpy as jnp
import numpy as np
from jax import lax
from jax.experimental import pallas as pl
from jax.experimental.pallas import tpu as pltpu
from jax.sharding import PartitionSpec as P

ITERS = 5
AXES = ("req", "mesh")
TAIL_ROW = 5
F32 = jnp.float32
BF16 = jnp.bfloat16


def rms_norm(values, gain):
    return values * lax.rsqrt(jnp.mean(values * values, axis=-1, keepdims=True) + 1e-05) * gain


def cost(flops, bytes_accessed):
    return pl.CostEstimate(flops=flops, bytes_accessed=bytes_accessed, transcendentals=0)


def in_hbm(values):
    return [pltpu.with_memory_space_constraint(value, pltpu.HBM) for value in values]


def in_vmem(values):
    return [pltpu.with_memory_space_constraint(value, pltpu.VMEM) for value in values]


def flip_req(bit, reqs, peers):
    return [(r * peers + z, (r ^ bit) * peers + z) for r in range(reqs) for z in range(peers)]


def shift_mesh(step, reqs, peers):
    return [(r * peers + z, r * peers + (z + step) % peers) for r in range(reqs) for z in range(peers)]


def flip_mesh(bit, reqs, peers):
    return [(r * peers + z, r * peers + (z ^ bit)) for r in range(reqs) for z in range(peers)]


def gather_rows(own, move, shifts, flips, beside):
    flip_x, flip_y = flips
    rows = own.shape[0]
    one = move(own, shifts[1])
    x_own, y_own = move(own, flip_x), move(own, flip_y)
    three = move(own, shifts[3])
    two = move(one, shifts[1])
    x_one, y_one = move(one, flip_x), move(one, flip_y)
    *results, three = beside(three, [x_own, y_own])
    (two,) = release_call([two], [x_one, y_one])
    rest = jnp.concatenate([three, two], axis=0)
    x_rest, y_rest = move(rest, flip_x), move(rest, flip_y)
    xy_own, xy_one = move(x_own, flip_y), move(y_one, flip_x)
    xy_three, xy_two = move(x_rest[:rows], flip_y), move(y_rest[rows:], flip_x)
    parts = []
    for o, part in ((0, own), (2, x_own), (4, y_own), (6, xy_own)):
        parts.append((part, [(o, 0)]))
    for o, part in ((0, one), (2, x_one), (4, y_one), (6, xy_one)):
        parts.append((part, [(o, 1)]))
    for o, part in ((0, rest), (2, x_rest), (4, y_rest)):
        parts.append((part, [(o, 3), (o, 2)]))
    parts.append((xy_three, [(6, 3)]))
    parts.append((xy_two, [(6, 2)]))
    return [part for part, _ in parts], [where for _, where in parts], results, two, [xy_three, xy_two]


def prep_kernel(heads, len_ref, rate_ref, tok_ref, gain_ref, wg_ref, *refs):
    gate_ref, up_ref, down_ref = refs[:3]
    ffn_ref, normed_ref, weight_ref, carried_ref, tw_ref, decay_ref = refs[-7:-1]
    stripe = down_ref.shape[1]
    if stripe % 128 == 0:
        ffn_ref[:, 0:stripe] = gate_ref[...]
        ffn_ref[:, stripe : 2 * stripe] = up_ref[...]
        ffn_ref[:, 2 * stripe :] = down_ref[...]
    else:
        ffn_ref[...] = jnp.zeros(ffn_ref.shape, BF16)
    requests = weight_ref.shape[0]
    rows = tok_ref.shape[0]
    length = rows // requests
    normed = rms_norm(tok_ref[...].astype(F32), gain_ref[...]).astype(BF16)
    normed_ref[...] = normed
    lane = lax.broadcasted_iota(jnp.int32, (256, 2 * heads), 0)
    column = lax.broadcasted_iota(jnp.int32, (256, 2 * heads), 1)
    chosen = (column == 2 * lane) | ((column == 2 * (lane - 128) + 1) & (lane >= 128))
    gates = jnp.dot(chosen.astype(F32).astype(BF16), wg_ref[...], preferred_element_type=F32)
    logits = lax.dot_general(
        normed, gates.astype(BF16), (((1,), (1,)), ((), ())), preferred_element_type=F32
    )
    rate_lane = lax.broadcasted_iota(jnp.int32, (1, 128), 1)
    rate = jnp.zeros((1, 128), F32)
    for h in range(heads):
        rate = jnp.where(rate_lane == h, rate_ref[h], rate)
    position = lax.broadcasted_iota(jnp.int32, (length, 128), 0)
    lane = lax.broadcasted_iota(jnp.int32, (length, 128), 1)
    slot = jnp.where(lane < length, lane, lane - length)
    causal = position >= slot
    below = lax.broadcasted_iota(jnp.int32, (length, length), 0) >= lax.broadcasted_iota(
        jnp.int32, (length, length), 1
    )
    below = below.astype(F32)
    for r in range(requests):
        mine = logits[r * length : (r + 1) * length]
        live = (position < len_ref[r]).astype(F32)
        beta = jax.nn.sigmoid(mine[:, :128]) * live
        forget = mine[:, 128:]
        softplus = jnp.maximum(forget, 0.0) + jnp.log1p(jnp.exp(-jnp.abs(forget)))
        log_decay = -rate * softplus * live
        cum = jnp.dot(
            below, log_decay, precision=lax.Precision.HIGHEST, preferred_element_type=F32
        )
        last = cum[length - 1 : length]
        cum_rows = jnp.concatenate([cum, cum], axis=0).T
        beta_rows = jnp.concatenate([beta, beta], axis=0).T
        carried = jnp.exp(cum)
        tail_weight = jnp.exp(last - cum) * beta
        decay = jnp.exp(last)
        for h in range(heads):
            spread = cum[:, h : h + 1] - cum_rows[h : h + 1]
            weight = jnp.where(causal, jnp.exp(jnp.minimum(spread, 0.0)), 0.0)
            weight_ref[r, h] = weight * beta_rows[h : h + 1]
            carried_ref[r, h] = jnp.broadcast_to(carried[:, h : h + 1], (length, 128))
            tw_ref[r, h] = jnp.broadcast_to(tail_weight[:, h : h + 1], (length, 128))
            decay_ref[r, h : h + 1] = jnp.broadcast_to(decay[:, h : h + 1], (1, 128))


def prep_call(lengths, decay_rate, tokens, gain, w_gates, ffn_weights, through, behind):
    rows, width = tokens.shape
    requests, heads = lengths.shape[0], decay_rate.shape[0]
    length = rows // requests
    smem = pl.BlockSpec(memory_space=pltpu.SMEM)
    hbm = pl.BlockSpec(memory_space=pltpu.HBM)
    whole = lambda shape: pl.BlockSpec(shape, lambda i: (0,) * len(shape))
    inputs = [tokens, gain.reshape(1, width), w_gates.T, *ffn_weights]
    hidden, stripe = ffn_weights[0].shape
    wide = (requests, heads, length, 128)
    shapes = [(hidden, 3 * stripe), (rows, width), wide, wide, wide, (requests, heads, 128)]
    return pl.pallas_call(
        functools.partial(prep_kernel, heads),
        grid=(1,),
        in_specs=[smem] * 2 + [whole(value.shape) for value in inputs] + [hbm] * (1 + len(behind)),
        out_specs=[whole(shape) for shape in shapes] + [hbm],
        out_shape=[pltpu.HBM(shape, F32 if i > 1 else BF16) for i, shape in enumerate(shapes)]
        + [pltpu.HBM(through.shape, through.dtype)],
        input_output_aliases={2 + len(inputs): len(shapes)},
        compiler_params=pltpu.CompilerParams(vmem_limit_bytes=20 << 20),
        cost_estimate=cost(3 << 30, 1 << 16),
        name="norm_gates",
    )(lengths, decay_rate, *in_hbm(inputs + [through] + behind))


def split_kernel(core_ref, w_ref, keep_ref, send_ref):
    wide = keep_ref.shape[1] // 3
    for which in range(3):
        to = slice(which * wide, (which + 1) * wide)
        for out_ref, half in ((keep_ref, core_ref[0]), (send_ref, 1 - core_ref[0])):
            begin = pl.multiple_of((2 * which + half) * wide, wide)
            out_ref[:, to] = w_ref[:, pl.ds(begin, wide)]


def split_call(core, weights):
    rows, columns = weights.shape
    vmem = pl.BlockSpec(memory_space=pltpu.VMEM)
    return pl.pallas_call(
        split_kernel,
        in_specs=[pl.BlockSpec(memory_space=pltpu.SMEM), vmem],
        out_specs=[vmem] * 2,
        out_shape=[jax.ShapeDtypeStruct((rows, columns // 2), BF16)] * 2,
        cost_estimate=cost(1 << 28, 1 << 16),
        name="split_heads",
    )(core, weights)


def project_kernel(n_pieces, spans, at_ref, x_ref, other_ref, *refs):
    pieces = refs[:n_pieces]
    mine_ref, theirs_ref, weights, sems = refs[-4:]
    step = pl.program_id(0)
    columns = mine_ref.shape[1]
    chunks = weights.shape[1] // columns

    def copies(c):
        cut = pl.ds(c * columns, columns)
        for i, (piece, first, rows) in enumerate(spans):
            begin = pl.multiple_of(at_ref[i], 16)
            yield pltpu.make_async_copy(
                pieces[piece].at[pl.ds(first, rows), cut],
                weights.at[pl.ds(begin, rows), cut],
                sems.at[c, i],
            )

    @pl.when(step == 0)
    def _():
        for c in range(chunks):
            for copy in copies(c):
                copy.start()

    for c in range(chunks):

        @pl.when(step == c)
        def _():
            for copy in copies(c):
                copy.wait()

    now = weights[:, pl.ds(pl.multiple_of(step * columns, columns), columns)]
    theirs = jnp.dot(other_ref[...], now, preferred_element_type=F32)
    theirs_ref[...] = theirs.astype(BF16)
    mine_ref[...] = jnp.dot(x_ref[...], now, preferred_element_type=F32).astype(BF16)


def project_call(at, spans, x, other, pieces, behind):
    rows, depth = x.shape
    columns = pieces[0].shape[1]
    wide = 512
    whole = pl.BlockSpec(x.shape, lambda j, s: (0, 0))
    block = pl.BlockSpec((rows, wide), lambda j, s: (0, j))
    return pl.pallas_call(
        functools.partial(project_kernel, len(pieces), spans),
        grid_spec=pltpu.PrefetchScalarGridSpec(
            num_scalar_prefetch=1,
            grid=(columns // wide,),
            in_specs=[whole, whole] + [pl.BlockSpec(memory_space=pltpu.HBM)] * len(pieces + behind),
            out_specs=[block, block],
            scratch_shapes=[
                pltpu.VMEM((depth, columns), BF16),
                pltpu.SemaphoreType.DMA((columns // wide, len(spans))),
            ],
        ),
        out_shape=[pltpu.HBM((rows, columns), BF16)] * 2,
        compiler_params=pltpu.CompilerParams(vmem_limit_bytes=16 << 20),
        cost_estimate=cost(3 << 30, 1 << 16),
        name="project",
    )(at, *in_hbm([x, other] + pieces + behind))


def conv_kernel(half_ref, len_ref, projected_ref, tail_ref, conv_ref, *refs):
    act_ref, new_tail_ref = refs[-2:]
    requests, window, columns = tail_ref.shape
    length = projected_ref.shape[0] // requests
    is_vector = pl.program_id(0) < 2
    for r in range(requests):
        blank = jnp.zeros((TAIL_ROW, columns), F32)
        head_rows = jnp.concatenate([blank, tail_ref[r].astype(F32)], axis=0)
        mine = projected_ref[r * length : (r + 1) * length].astype(F32)
        extended = jnp.concatenate([head_rows, mine], axis=0)
        wanted = lax.broadcasted_iota(jnp.int32, (8, extended.shape[0]), 0) + len_ref[r]
        place = lax.broadcasted_iota(jnp.int32, (8, extended.shape[0]), 1)
        chosen = (place == wanted + TAIL_ROW).astype(F32)
        rows = jnp.dot(chosen, extended, preferred_element_type=F32)
        new_tail_ref[r] = rows[:window].astype(BF16)
        total = conv_ref[0:1] * extended[TAIL_ROW : TAIL_ROW + length]
        for tap in range(1, window + 1):
            total = total + conv_ref[tap : tap + 1] * extended[
                TAIL_ROW + tap : TAIL_ROW + tap + length
            ]
        act = total * jax.nn.sigmoid(total)
        for h in range(columns // 128):
            head = act[:, h * 128 : (h + 1) * 128]
            scale = lax.rsqrt(jnp.sum(head * head, axis=-1, keepdims=True) + 1e-06)
            scale = jnp.where(is_vector, scale, jnp.ones_like(scale))
            act_ref[r * length : (r + 1) * length, h * 128 : (h + 1) * 128] = head * scale


def conv_call(half, lengths, projected, tails, conv_weight, held):
    rows, columns = projected.shape
    requests, window = tails.shape[:2]
    wide = columns // 3
    rows_block = pl.BlockSpec((rows, wide), lambda j, s, t: (0, 2 * j + s[0]))
    tail_block = pl.BlockSpec((requests, window, wide), lambda j, s, t: (0, 0, 2 * j + s[0]))
    return pl.pallas_call(
        conv_kernel,
        grid_spec=pltpu.PrefetchScalarGridSpec(
            num_scalar_prefetch=2,
            grid=(3,),
            in_specs=[
                pl.BlockSpec((rows, wide), lambda j, s, t: (0, j)),
                tail_block,
                pl.BlockSpec((window + 1, wide), lambda j, s, t: (0, 2 * j + s[0])),
            ]
            + [pl.BlockSpec(memory_space=pl.ANY)] * len(held),
            out_specs=[rows_block, tail_block],
        ),
        out_shape=[
            pltpu.HBM((rows, 2 * columns), F32),
            pltpu.HBM(tails.shape, BF16),
        ],
        input_output_aliases={5: 0, 6: 1} if held else {},
        compiler_params=pltpu.CompilerParams(vmem_limit_bytes=16 << 20),
        cost_estimate=cost(2 << 30, 1 << 16),
        name="conv_norm",
    )(half, lengths, *in_hbm([projected, tails, conv_weight] + held))


def stats_kernel(heads, place_ref, slot_ref, k_ref, v_ref, tw_ref, fd_ref, s_ref, vs_ref, *refs):
    tail_ref, out_ref = refs
    size = 128
    row = lax.broadcasted_iota(jnp.int32, (size, size), 0)
    col = lax.broadcasted_iota(jnp.int32, (size, size), 1)
    half = heads // 2
    contract = (((0,), (0,)), ((), ()))
    keys_end = []
    for h in range(heads):
        keys = k_ref[:, h * size : (h + 1) * size]
        values = v_ref[:, h * size : (h + 1) * size]
        tail_weight = tw_ref[0, h]
        both = jnp.concatenate([keys * tail_weight, values * tail_weight], axis=1).astype(BF16)
        sums = lax.dot_general(both, keys.astype(BF16), contract, preferred_element_type=F32)
        decay = fd_ref[0, h : h + 1]
        keys_end.append(decay * s_ref[0, h] + sums[:size])
        at = half * size + h * size
        out_ref[0, at : at + size] = (decay * vs_ref[0, h] + sums[size:]).astype(BF16)
    diagonals = []
    for p in range(half):
        low, high = keys_end[p], keys_end[p + half]
        out_ref[0, p * size : (p + 1) * size] = jnp.where(row >= col, low, high).astype(BF16)
        diagonals.append(jnp.sum(jnp.where(row == col, high, 0.0), axis=0, keepdims=True))
    at = (half + heads) * size
    slot = slot_ref[pl.program_id(0)].astype(F32)
    diagonals.append(jnp.full((16 - half, size), slot, F32))
    out_ref[0, at : at + 16] = jnp.concatenate(diagonals, axis=0).astype(BF16)
    tail = tail_ref[0].astype(F32)
    strips = [tail[:, c : c + size] for c in range(0, tail.shape[1], size)]
    fill = out_ref.shape[1] - at - 16 - len(strips) * tail.shape[0]
    strips.append(jnp.zeros((fill, size), F32))
    out_ref[0, at + 16 :] = jnp.concatenate(strips, axis=0).astype(BF16)


def stats_call(places, slots, act, tail_weight, decay, keys_start, values_start, tails):
    requests, heads = keys_start.shape[:2]
    length, width = act.shape[0] // requests, heads * 128
    tail_rows = tails.shape[1] * tails.shape[2] // 128
    out_rows = (heads // 2 + heads) * 128 + 16 + tail_rows + -tail_rows % 16
    matrices = pl.BlockSpec((1, heads, 128, 128), lambda i, s, t: (i, 0, 0, 0))
    return pl.pallas_call(
        functools.partial(stats_kernel, heads),
        grid_spec=pltpu.PrefetchScalarGridSpec(
            num_scalar_prefetch=2,
            grid=(requests,),
            in_specs=[
                pl.BlockSpec((length, width), lambda i, s, t: (i, 1)),
                pl.BlockSpec((length, width), lambda i, s, t: (i, 2)),
                pl.BlockSpec((1, heads, length, 128), lambda i, s, t: (i, 0, 0, 0)),
                pl.BlockSpec((1, heads, 128), lambda i, s, t: (i, 0, 0)),
                matrices,
                matrices,
                pl.BlockSpec((1,) + tails.shape[1:], lambda i, s, t: (i, 0, 0)),
            ],
            out_specs=pl.BlockSpec((1, out_rows, 128), lambda i, s, t: (s[i], 0, 0)),
        ),
        out_shape=pltpu.HBM((requests, out_rows, 128), BF16),
        compiler_params=pltpu.CompilerParams(vmem_limit_bytes=16 << 20),
        cost_estimate=cost(3 << 30, 1 << 16),
        name="stats",
    )(
        places,
        slots,
        *in_hbm([act, act, tail_weight, decay, keys_start, values_start, tails]),
    )


def unpack_kernel(heads, part_ref, *refs):
    keys_ref, values_ref, tail_ref, keys_buf, values_buf, tail_buf, sems = refs[-7:]
    size = 128
    half = heads // 2
    window, columns = tail_ref.shape[1:]
    row = lax.broadcasted_iota(jnp.int32, (size, size), 0)
    col = lax.broadcasted_iota(jnp.int32, (size, size), 1)
    n_parts = part_ref.shape[0]
    under_way = []
    for s in range(n_parts):
        buf = s % 2
        if s >= 2:
            for copy in under_way[s - 2]:
                copy.wait()
        at = (half + heads) * size
        diagonals = part_ref[s, at : at + 16].astype(F32)
        slot = jnp.max(diagonals[half : half + 1]).astype(jnp.int32)
        for p in range(half):
            packed = part_ref[s, p * size : (p + 1) * size].astype(F32)
            turned = packed.T
            keys_buf[buf, p] = jnp.where(row >= col, packed, turned)
            keys_buf[buf, p + half] = jnp.where(
                row < col, packed, jnp.where(row == col, diagonals[p : p + 1], turned)
            )
        for h in range(heads):
            begin = (half + h) * size
            values_buf[buf, h] = part_ref[s, begin : begin + size].astype(F32)
        rows = part_ref[s, at + 16 :].astype(F32)
        strips = [rows[c * window : (c + 1) * window] for c in range(columns // size)]
        tail_buf[s] = jnp.concatenate(strips, axis=1).astype(BF16)
        copies = [
            pltpu.make_async_copy(keys_buf.at[buf], keys_ref.at[slot], sems.at[s, 0]),
            pltpu.make_async_copy(values_buf.at[buf], values_ref.at[slot], sems.at[s, 1]),
            pltpu.make_async_copy(tail_buf.at[s], tail_ref.at[slot], sems.at[s, 2]),
        ]
        for copy in copies:
            copy.start()
        under_way.append(copies)
    for copies in under_way[-2:]:
        for copy in copies:
            copy.wait()


def unpack_call(parts, heads, tail_shape, behind):
    n_parts = parts.shape[0]
    vmem = pl.BlockSpec(memory_space=pltpu.VMEM)
    hbm = pl.BlockSpec(memory_space=pltpu.HBM)
    matrices = jax.ShapeDtypeStruct((n_parts, heads, 128, 128), F32)
    return pl.pallas_call(
        functools.partial(unpack_kernel, heads),
        in_specs=[vmem] + [pl.BlockSpec(memory_space=pl.ANY)] * len(behind),
        out_specs=[hbm, hbm, hbm],
        out_shape=[matrices, matrices, jax.ShapeDtypeStruct((n_parts,) + tail_shape, BF16)],
        scratch_shapes=[
            pltpu.VMEM((2, heads, 128, 128), F32),
            pltpu.VMEM((2, heads, 128, 128), F32),
            pltpu.VMEM((n_parts,) + tail_shape, BF16),
            pltpu.SemaphoreType.DMA((n_parts, 3)),
        ],
        compiler_params=pltpu.CompilerParams(vmem_limit_bytes=16 << 20),
        cost_estimate=cost(3 << 30, 1 << 16),
        name="unpack",
    )(parts, *in_hbm(behind))


def two_terms(values):
    high = values.astype(BF16)
    low = (values - high.astype(F32)).astype(BF16)
    return high, low


def lane_sum(values):
    return jnp.sum(values, axis=-1, keepdims=True)


def cg_kernel(heads, group, ridge_ref, q_ref, k_ref, v_ref, w_ref, c_ref, s_ref, vs_ref, *refs):
    out_ref = refs[-1]
    size = 128
    part = lambda ref, h: ref[:, h * size : (h + 1) * size]
    first_half = lax.broadcasted_iota(jnp.int32, (q_ref.shape[0], size), 1) < size // 2
    transposed = (((1,), (1,)), ((), ()))
    for base in range(0, heads, group):
        hs = range(base, base + group)
        keys = [part(k_ref, h) for h in hs]
        keys2 = [jnp.concatenate([k, k], axis=0) for k in keys]
        keys2_bf = [k.astype(BF16) for k in keys2]
        keys_t = [k.T.astype(BF16) for k in keys2]
        system = []
        for i, h in enumerate(hs):
            m = jnp.concatenate([s_ref[0, h].astype(BF16), keys_t[i]], axis=1)
            system.append(m)

        def both_terms(field):
            return jnp.concatenate(two_terms(field), axis=0)

        def joined(products):
            rows = products.shape[0] // 2
            return products[:rows] + products[rows:]

        def scored(products, i, h):
            scores = products[:, size:] * w_ref[0, h]
            high = scores.astype(BF16).astype(F32)
            return jnp.where(first_half, high, scores - high).astype(BF16)

        direction = [part(q_ref, h) for h in hs]
        residual = list(direction)
        total = [None] * group
        norm = [lane_sum(r * r) for r in residual]
        for it in range(ITERS):
            products = [
                joined(jnp.dot(both_terms(direction[i]), system[i], preferred_element_type=F32))
                for i in range(group)
            ]
            spread = [
                jnp.dot(scored(products[i], i, h), keys2_bf[i], preferred_element_type=F32)
                for i, h in enumerate(hs)
            ]
            for i, h in enumerate(hs):
                applied = (
                    c_ref[0, h] * products[i][:, :size] + spread[i] + ridge_ref[h] * direction[i]
                )
                step = norm[i] / (lane_sum(direction[i] * applied) + 1e-20)
                moved = step * direction[i]
                total[i] = moved if total[i] is None else total[i] + moved
                if it + 1 < ITERS:
                    residual[i] = residual[i] - step * applied
                    following = lane_sum(residual[i] * residual[i])
                    direction[i] = residual[i] + following / (norm[i] + 1e-20) * direction[i]
                    norm[i] = following
        for i, h in enumerate(hs):
            start_m = jnp.concatenate([vs_ref[0, h].astype(BF16), keys2_bf[i]], axis=0)
            products = joined(
                lax.dot_general(
                    both_terms(total[i]), start_m, transposed, preferred_element_type=F32
                )
            )
            values = part(v_ref, h)
            values2 = jnp.concatenate([values, values], axis=0).astype(BF16)
            read = c_ref[0, h] * products[:, :size] + jnp.dot(
                scored(products, i, h), values2, preferred_element_type=F32
            )
            out_ref[:, h * size : (h + 1) * size] = read.astype(BF16)


def cg_call(ridge, act, weight2, carried, keys_start, values_start, first, count, held, behind):
    requests, heads = keys_start.shape[:2]
    length, width = act.shape[0] // requests, heads * 128
    per_head = lambda rows: pl.BlockSpec((1, heads, rows, 128), lambda i: (i + first, 0, 0, 0))
    rows_of = lambda which: pl.BlockSpec((length, width), lambda i: (i + first, which))
    inputs = [act, act, act, weight2, carried, keys_start, values_start] + held + behind
    return pl.pallas_call(
        functools.partial(cg_kernel, heads, 8),
        grid=(count,),
        in_specs=[pl.BlockSpec(memory_space=pltpu.SMEM)]
        + [rows_of(0), rows_of(1), rows_of(2)]
        + [per_head(length), per_head(length), per_head(128), per_head(128)]
        + [pl.BlockSpec(memory_space=pl.ANY)] * len(held + behind),
        out_specs=rows_of(0),
        out_shape=jax.ShapeDtypeStruct((requests * length, width), BF16),
        input_output_aliases={8: 0} if held else {},
        compiler_params=pltpu.CompilerParams(vmem_limit_bytes=20 << 20),
        cost_estimate=cost(4 << 30, 1 << 16),
        name="cg",
    )(ridge, *in_hbm(inputs))


def release_kernel(*refs):
    del refs


def release_call(values, behind):
    hbm = pl.BlockSpec(memory_space=pltpu.HBM)
    return pl.pallas_call(
        release_kernel,
        in_specs=[hbm] * len(values) + [pl.BlockSpec(memory_space=pl.ANY)] * len(behind),
        out_specs=[hbm] * len(values),
        out_shape=[pltpu.HBM(value.shape, value.dtype) for value in values],
        input_output_aliases={i: i for i in range(len(values))},
        cost_estimate=cost(1 << 26, 1 << 10),
        name="release",
    )(*in_hbm(values + behind))


def out_kernel(x_ref, tok_ref, gain_ref, w_ref, *refs):
    after_ref, in_ref = refs[-2:]
    attended = jnp.dot(x_ref[...], w_ref[...], preferred_element_type=F32)
    after_attn = (tok_ref[...].astype(F32) + attended).astype(BF16)
    after_ref[...] = after_attn
    in_ref[...] = rms_norm(after_attn.astype(F32), gain_ref[...]).astype(BF16)


def out_call(head_rows, tokens, first, gain, weights, behind):
    rows, width = head_rows.shape[0] // 2, tokens.shape[1]
    half = lambda a: pl.BlockSpec((rows, a.shape[1]), lambda i: (first, 0))
    whole = lambda a: pl.BlockSpec(a.shape, lambda i: (0, 0))
    return pl.pallas_call(
        out_kernel,
        grid=(1,),
        in_specs=[
            half(head_rows),
            half(tokens),
            whole(gain),
            whole(weights),
        ]
        + [pl.BlockSpec(memory_space=pl.ANY)] * len(behind),
        out_specs=[pl.BlockSpec((rows, width), lambda i: (0, 0))] * 2,
        out_shape=[jax.ShapeDtypeStruct((rows, width), BF16)] * 2,
        compiler_params=pltpu.CompilerParams(vmem_limit_bytes=16 << 20),
        cost_estimate=cost(2 << 30, 1 << 16),
        name="out_proj",
    )(*in_hbm([head_rows, tokens, gain, weights] + behind))


def ffn_rows(x, matrices, ready):
    gate_w, up_w, down_w = matrices
    turned = (((1,), (1,)), ((), ()))
    total = None
    for block in range(gate_w.shape[0]):
        ready(block, 0)
        gate = lax.dot_general(x, gate_w[block], turned, preferred_element_type=F32)
        ready(block, 1)
        up = lax.dot_general(x, up_w[block], turned, preferred_element_type=F32)
        hidden = (gate * jax.nn.sigmoid(gate) * up).astype(BF16)
        ready(block, 2)
        sums = jnp.dot(hidden, down_w[block], preferred_element_type=F32)
        total = sums if total is None else total + sums
    return total


def ffn_first_kernel(spans, counts, order_ref, *refs):
    n_in, n_pieces, n_out = counts
    inputs, pieces = refs[:n_in], refs[n_in : n_in + n_pieces]
    outputs, matrices, sems = refs[-4 - n_out : -4], refs[-4:-1], refs[-1]
    size = 128

    def copies(block, which):
        for i, (piece, j) in enumerate(spans[block]):
            to = pl.ds(pl.multiple_of(order_ref[j] * size, size), size)
            yield pltpu.make_async_copy(
                pieces[piece].at[:, pl.ds(which * size, size)],
                matrices[which].at[block, :, to],
                sems.at[block, which, i],
            )

    for block in range(len(spans)):
        for which in range(3):
            for copy in copies(block, which):
                copy.start()

    def ready(block, which):
        for copy in copies(block, which):
            copy.wait()

    x = jnp.concatenate([ref[...] for ref in inputs], axis=0)
    total = ffn_rows(x, matrices, ready)
    begin = 0
    for out_ref in outputs:
        rows = out_ref.shape[0]
        out_ref[...] = total[begin : begin + rows].astype(out_ref.dtype)
        begin += rows


def ffn_first_call(order, spans, inputs, pieces, outputs):
    width = inputs[0].shape[1]
    hidden = pieces[0].shape[0]
    vmem = pl.BlockSpec(memory_space=pltpu.VMEM)
    matrix = pltpu.VMEM((len(spans), hidden, width), BF16)
    counts = (len(inputs), len(pieces), len(outputs))
    return pl.pallas_call(
        functools.partial(ffn_first_kernel, spans, counts),
        grid_spec=pltpu.PrefetchScalarGridSpec(
            num_scalar_prefetch=1,
            grid=(),
            in_specs=[vmem] * len(inputs)
            + [pl.BlockSpec(memory_space=pltpu.HBM)] * len(pieces),
            out_specs=[vmem] * (len(outputs) + 3),
            scratch_shapes=[pltpu.SemaphoreType.DMA((len(spans), 3, len(spans[0])))],
        ),
        out_shape=[jax.ShapeDtypeStruct((rows, width), kind) for rows, kind in outputs]
        + [matrix] * 3,
        compiler_params=pltpu.CompilerParams(vmem_limit_bytes=20 << 20),
        cost_estimate=cost(5 << 30, 1 << 16),
        name="ffn_first",
    )(order, *inputs, *in_hbm(pieces))


def ffn_second_kernel(counts, *refs):
    n_in, n_out = counts
    matrices, outputs = refs[n_in : n_in + 3], refs[-n_out:]
    x = jnp.concatenate([ref[...] for ref in refs[:n_in]], axis=0)
    total = ffn_rows(x, matrices, lambda block, which: None)
    begin = 0
    for out_ref in outputs:
        rows = out_ref.shape[0]
        out_ref[...] = total[begin : begin + rows].astype(out_ref.dtype)
        begin += rows


def ffn_second_call(inputs, matrices, kind, behind):
    vmem = pl.BlockSpec(memory_space=pltpu.VMEM)
    return pl.pallas_call(
        functools.partial(ffn_second_kernel, (len(inputs), len(inputs))),
        in_specs=[vmem] * (len(inputs) + 3)
        + [pl.BlockSpec(memory_space=pl.ANY)] * len(behind),
        out_specs=[vmem] * len(inputs),
        out_shape=[jax.ShapeDtypeStruct(x.shape, kind) for x in inputs],
        compiler_params=pltpu.CompilerParams(vmem_limit_bytes=16 << 20),
        cost_estimate=cost(3 << 30, 1 << 16),
        name="ffn_second",
    )(*inputs, *in_vmem(matrices), *in_hbm(behind))


def sum_kernel(*refs):
    out_ref = refs[-1]
    begin = 0
    for i in range(0, len(refs) - 1, 3):
        after_ref, mine_ref, got_ref = refs[i : i + 3]
        rows = after_ref.shape[0]
        total = after_ref[...].astype(F32) + (mine_ref[...] + got_ref[...].astype(F32))
        out_ref[begin : begin + rows] = total.astype(BF16)
        begin += rows


def sum_call(values):
    vmem = pl.BlockSpec(memory_space=pltpu.VMEM)
    rows = sum(value.shape[0] for value in values[::3])
    return pl.pallas_call(
        sum_kernel,
        in_specs=[vmem] * len(values),
        out_specs=vmem,
        out_shape=jax.ShapeDtypeStruct((rows, values[0].shape[1]), BF16),
        compiler_params=pltpu.CompilerParams(vmem_limit_bytes=8 << 20),
        cost_estimate=cost(1 << 30, 1 << 16),
        name="last_sum",
    )(*values)


def shards(
    tokens,
    lengths,
    ridge_keys,
    ridge_values,
    conv_tail,
    page_table,
    w_qkv,
    conv_weight,
    w_gates,
    decay_rate,
    ridge,
    w_out,
    attn_gain,
    ffn_gain,
    w_gate,
    w_up,
    w_down,
):
    requests, length, width = tokens.shape
    heads = decay_rate.shape[0]
    row_count = requests * length
    reqs, peers = lax.axis_size("req"), lax.axis_size("mesh")
    my_req, my_mesh = lax.axis_index("req"), lax.axis_index("mesh")
    move = lambda value, pairs: lax.ppermute(value, AXES, pairs)
    hop_one, hop_two = flip_mesh(1, reqs, peers), flip_mesh(2, reqs, peers)
    own_rows = w_qkv.shape[0]

    w_out_all = lax.all_gather(w_out, AXES, axis=0, tiled=True)
    flat_tokens = tokens.reshape(row_count, width)
    prep = functools.partial(
        prep_call,
        lengths,
        decay_rate,
        flat_tokens,
        attn_gain,
        w_gates,
        [w_gate.T, w_up.T, w_down],
    )
    ordered = (reqs, peers) == (8, 4)
    core = (my_req % 2).astype(jnp.int32).reshape(1)
    if ordered:
        shifts = {s: shift_mesh(s, reqs, peers) for s in range(1, peers)}
        flips = [flip_req(bit, reqs, peers) for bit in (1, 2, 4)]
        keep, send = split_call(core, w_qkv)
        chip_rows = jnp.concatenate([keep, move(send, flips[0])], axis=0)
        qkv_pieces, places, results, two, last = gather_rows(
            chip_rows, move, shifts, flips[1:], prep
        )
        ffn_own, *prepared = results
        spans, listed = [], []
        for piece, chips in enumerate(places):
            for i, (o, s) in enumerate(chips):
                for other in (0, 1):
                    spans.append((piece, (2 * i + other) * own_rows, own_rows))
                    listed.append((o ^ other, s))
        listed = np.array(listed, np.int32)
        owner = (my_req ^ listed[:, 0]) * peers + (my_mesh - listed[:, 1]) % peers
        qkv_at = (owner * own_rows).astype(jnp.int32)
        ffn_two = move(ffn_own, hop_two)
        (ffn_own,) = release_call([ffn_own], last)
        x_own, y_own = move(ffn_own, flips[1]), move(ffn_own, flips[2])
        normed, weight2, carried, tail_weight, decay = prepared
        mine, theirs = project_call(
            qkv_at, spans, normed, move(normed, flips[0]), qkv_pieces, [ffn_two]
        )
        got = move(theirs, flips[0])
        (ffn_two,) = release_call([ffn_two], [theirs])
        x_two, y_two = move(ffn_two, flips[1]), move(ffn_two, flips[2])
    else:
        w_qkv_all = lax.all_gather(w_qkv, AXES, axis=0, tiled=True)
        qkv_pieces = list(split_call(core, w_qkv_all))
        spans = [(0, 0, w_qkv_all.shape[0])]
        qkv_at = jnp.zeros((1,), jnp.int32)
        _, normed, weight2, carried, tail_weight, decay, _ = prep(w_out, [])
        mine, _ = project_call(qkv_at, spans, normed, normed, qkv_pieces[:1], [])
        got, _ = project_call(qkv_at, spans, normed, normed, qkv_pieces[1:], [])
        gate_all = lax.all_gather(w_gate, "req", axis=0, tiled=True)
        up_all = lax.all_gather(w_up, "req", axis=0, tiled=True)
        down_all = lax.all_gather(w_down, "req", axis=1, tiled=True)
        stripes = width // 128
        ffn_pieces = []
        for j in range(stripes):
            cut = slice(j * 128, (j + 1) * 128)
            piece = jnp.concatenate([gate_all[cut].T, up_all[cut].T, down_all[:, cut]], axis=1)
            ffn_pieces.append(piece)
        ffn_pieces = ffn_pieces + [move(piece, hop_two) for piece in ffn_pieces]
        ffn_spans = [[(i * stripes + j, j) for j in range(stripes)] for i in (0, 1)]
        ffn_order = jnp.arange(stripes)

    held = conv_call(core, lengths, mine, conv_tail, conv_weight, [])
    act, new_tail = conv_call(1 - core, lengths, got, conv_tail, conv_weight, list(held))

    packed = stats_call(
        page_table // requests,
        page_table % requests,
        act,
        tail_weight,
        decay,
        ridge_keys,
        ridge_values,
        new_tail,
    )
    if ordered:
        xy_own, xy_two = move(x_own, flips[2]), move(y_two, flips[1])
        ffn_pieces = [ffn_own, x_own, y_own, xy_own, ffn_two, x_two, y_two, xy_two]
        ffn_pieces = ffn_pieces + [move(p, flips[0]) for p in ffn_pieces]
        ffn_order = my_req ^ np.array((0, 2, 4, 6, 1, 3, 5, 7), np.int32)
        ffn_spans = [
            [(4 * i + j, j) for j in range(4)] + [(8 + 4 * i + j, 4 + j) for j in range(4)]
            for i in (0, 1)
        ]
        behind_a = [x_own, y_own]
        behind_b = [x_two, y_two, xy_own, *ffn_pieces[8:11], ffn_pieces[12]]
        behind_out = [xy_two, ffn_pieces[11], *ffn_pieces[13:15]]
    else:
        behind_a, behind_b, behind_out = [], [], []
    ffn_order = ffn_order.astype(jnp.int32)

    parts = lax.all_to_all(packed, "mesh", split_axis=0, concat_axis=0, tiled=True)

    per = requests // 2
    part_rows = per * length
    gain = ffn_gain.reshape(1, width)
    system = (ridge, act, weight2, carried, ridge_keys, ridge_values)
    heads_a = cg_call(*system, 0, per, [], [packed] + behind_a)
    after_a, in_a = out_call(heads_a, flat_tokens, 0, gain, w_out_all, [])
    theirs_a = move(in_a, hop_one)
    heads_b = cg_call(*system, per, per, [heads_a], [in_a] + behind_b)
    after_b, in_b = out_call(heads_b, flat_tokens, 1, gain, w_out_all, behind_out)
    theirs_b = move(in_b, hop_one)
    for_a, *matrices = ffn_first_call(
        ffn_order, ffn_spans, [theirs_a], ffn_pieces, [(part_rows, BF16)]
    )
    got_a = move(for_a, hop_one)
    (for_b,) = ffn_second_call([theirs_b], matrices, BF16, [for_a])
    got_b = move(for_b, hop_one)
    mine_a, mine_b = ffn_second_call([in_a, in_b], matrices, F32, [for_b])
    keys_decode, values_decode, tail_decode = unpack_call(
        parts, heads, conv_tail.shape[1:], [mine_b]
    )
    mixed = sum_call([after_a, mine_a, got_a, after_b, mine_b, got_b])
    return (
        mixed.reshape(requests, length, width),
        keys_decode,
        values_decode,
        tail_decode,
        heads_b.reshape(requests, length, -1),
    )


def solution(mesh):
    rows = P(AXES)
    in_specs = (
        rows,
        rows,
        rows,
        rows,
        rows,
        rows,
        rows,
        P(),
        P(),
        P(),
        P(),
        rows,
        P(),
        P(),
        P("req", "mesh"),
        P("req", "mesh"),
        P("mesh", "req"),
    )
    out_specs = (rows, rows, rows, rows, rows)
    return jax.shard_map(shards, mesh=mesh, in_specs=in_specs, out_specs=out_specs, check_vma=False)
```
